32 devices in a mesh: row: 4 (over x, core), col: 8 (over z, y).
Axes of the slice: x: 2, y: 2, z: 4, core: 2. Of those that a mesh axis runs over, the one named last changes fastest.
Arguments:
- features: bfloat16 [16384, 1024], P(('row', 'col')), may hold values from -6 to 6
- neighbours: int32 [16384, 16], P(('row', 'col')), may hold values from 0 to 1279, as said below
- degrees: int32 [16384], P(('row', 'col')), may hold values from 1 to 16, as said below
- send_rows: int32 [32, 512], P(('row', 'col')), may hold values from 0 to 511
- send_count: int32 [32, 32], P(('row', 'col')), may hold values from 8 to 16, as said below
- hub_rows: int32 [256], P(('row', 'col')), may hold values from 0 to 511, as said below
- w_self: bfloat16 [1024, 1024], replicated, may hold values from -0.1875 to 0.1875
- w_neigh: bfloat16 [1024, 1024], replicated, may hold values from -0.1875 to 0.1875
- bias_term: float32 [1024], replicated, may hold values from -3 to 3
- cotangent: bfloat16 [16384, 1024], P(('row', 'col')), may hold values from -6 to 6
Outputs:
- hidden: bfloat16 [16384, 1024], P(('row', 'col'))
- grad_x: bfloat16 [16384, 1024], P(('row', 'col'))
- grad_self: bfloat16 [1024, 1024], replicated
- grad_neigh: bfloat16 [1024, 1024], replicated
The draws below stay inside these ranges and needn't reach their ends.
Inputs may be any that keep to these rules, and one draw needn't show every extreme that they name: neighbours of partition d point to its own rows (below 512), to live slots of arrived_d only (row 512 + p * 16 + s with p != d and s < send_count[p, d]), or to hub rows; entries at j >= degrees[i] also lie in the table. `degrees`: every seed has at least one neighbour. `send_count`: each partition sends between 8 and 16 live rows to each partition, and exactly 16 to the next one. `hub_rows`: the 8 hub rows of a partition are distinct.
All inputs are finite; a program needn't handle non-finite values.
Results may differ from the reference program's by a relative error of at most 0.0064.
Values may be sent and summed in bfloat16 or wider, within the bound.
No kernel may reach another device: no remote copies, remote signals or barrier semaphores. Data moves between devices by JAX's collectives and lax.ppermute only.
A program may use at most 128 MiB of HBM per device.

```python
import jax
import jax.numpy as jnp
from jax import lax

D = 1024
NODE_DEV = 512
FANOUT = 16
CAP = 16
HUB_DEV = 8
PEERS = 32
NODES = 16384
HUBS = 256
SLOTS = 512
N_ROW = 4
N_COL = 8


def count_table(key):
    n_dev = NODES // NODE_DEV
    base_key = jax.random.fold_in(key, 11)
    low_count = CAP // 2
    counts = low_count + jax.random.randint(base_key, (n_dev, n_dev), 0, CAP - low_count + 1)
    dev_ids = jnp.arange(n_dev, dtype=jnp.int32)
    next_one = (dev_ids[:, None] + 1) % n_dev == dev_ids[None, :]
    return jnp.where(next_one, CAP, counts).astype(jnp.int32)


def draw_send_count(key, part):
    return count_table(key)


def draw_neighbours(key, part):
    n_dev = NODES // NODE_DEV
    counts = count_table(key)
    base_key = jax.random.fold_in(key, 23)
    sub_keys = jax.random.split(base_key, 6)
    shape = (NODES, FANOUT)
    owner_dev = (jnp.arange(NODES, dtype=jnp.int32) // NODE_DEV)[:, None] * jnp.ones(shape, jnp.int32)
    pick_kind = jax.random.randint(sub_keys[0], shape, 0, 8)
    local_ids = jax.random.randint(sub_keys[1], shape, 0, NODE_DEV)
    offset = jax.random.randint(sub_keys[2], shape, 1, n_dev)
    peer_dev = (owner_dev + offset) % n_dev
    slot_limit = counts[peer_dev, owner_dev]
    slot_ids = jax.random.randint(sub_keys[3], shape, 0, slot_limit)
    remote_ids = NODE_DEV + peer_dev * CAP + slot_ids
    hub_first = jax.random.randint(sub_keys[4], shape, 0, HUBS)
    hub_second = jax.random.randint(sub_keys[5], shape, 0, HUBS)
    hub_ids = NODE_DEV + n_dev * CAP + hub_first * hub_second // HUBS
    chosen = jnp.where(pick_kind < 4, local_ids, jnp.where(pick_kind < 6, remote_ids, hub_ids))
    chosen = chosen.at[0, 0].set(NODE_DEV + n_dev * CAP + HUBS - 1)
    chosen = chosen.at[0, 1].set(0)
    return chosen.astype(jnp.int32)


def draw_degrees(key, part):
    base_key = jax.random.fold_in(key, 37)
    drawn = jax.random.randint(base_key, (NODES,), 1, FANOUT + 1)
    return drawn.at[0].set(FANOUT).astype(jnp.int32)


def draw_hub_rows(key, part):
    n_dev = NODES // NODE_DEV
    base_key = jax.random.fold_in(key, 41)
    perm_key, shift_key = jax.random.split(base_key)
    sub_keys = jax.random.split(perm_key, n_dev)
    shifts = jax.random.randint(shift_key, (n_dev,), 0, NODE_DEV)
    shifts = shifts.at[0].set(0).at[1].set(NODE_DEV - 1)

    def one_part(one_key, shift):
        perm = jax.random.permutation(one_key, NODE_DEV)
        return ((perm - perm[0] + shift) % NODE_DEV)[:HUB_DEV]
    chosen = jax.vmap(one_part)(sub_keys, shifts)
    return chosen.reshape(-1).astype(jnp.int32)


def plant(entries, rng, least, top_value):
    dims = entries.shape
    place = [jax.random.randint(jax.random.fold_in(rng, axis), (), 0, dims[axis]) for axis in range(len(dims))]
    entries = entries.at[tuple(place)].set(least)
    longest = dims.index(max(dims))
    place[longest] = (place[longest] + 1) % dims[longest]
    return entries.at[tuple(place)].set(top_value)


def levels(stream_key, dims, shards, low, high):
    def one(axis_at, shards_of):
        steps = jax.random.uniform(jax.random.fold_in(jax.random.fold_in(stream_key, 6), axis_at), (shards_of,), jnp.float32, low / len(shards), high / len(shards))
        return jnp.repeat(jnp.exp(steps), dims[axis_at] // shards_of).reshape((-1,) + (1,) * (len(dims) - axis_at - 1))

    level = one(*shards[0])
    for cut in shards[1:]:
        level = level * one(*cut)
    return level


def bell_draw(stream_key, dims, spread, reach, shards=(), kind=jnp.bfloat16):
    values = jax.random.normal(stream_key, dims, jnp.float32) * spread
    if len(shards) > 0:
        values = levels(stream_key, dims, shards, -0.22, 0.18) * values
    return jnp.clip(values, min=-reach, max=reach).astype(kind)


def setup_inputs(seed: int = 0) -> dict:
    streams_of = jax.random.split(jax.random.key(seed), 11)
    features = bell_draw(streams_of[0], (NODES, D), 1.0, 6.0, ((0, 32),))
    neighbours = draw_neighbours(jax.random.fold_in(streams_of[10], 71), 0)
    degrees = draw_degrees(jax.random.fold_in(streams_of[10], 71), 0)
    send_rows = plant(jax.random.randint(streams_of[3], (PEERS, SLOTS), 0, NODE_DEV), jax.random.fold_in(streams_of[3], 1), 0, NODE_DEV - 1).astype(jnp.int32)
    send_count = draw_send_count(jax.random.fold_in(streams_of[10], 71), 0)
    hub_rows = draw_hub_rows(jax.random.fold_in(streams_of[10], 71), 0)
    w_self = bell_draw(streams_of[6], (D, D), D ** -0.5, 0.1875)
    w_neigh = bell_draw(streams_of[7], (D, D), D ** -0.5, 0.1875)
    bias_term = bell_draw(streams_of[8], (D,), 0.5, 3.0, (), jnp.float32)
    cotangent = bell_draw(streams_of[9], (NODES, D), 1.0, 6.0, ((0, 32),))
    return {"features": features, "neighbours": neighbours, "degrees": degrees, "send_rows": send_rows, "send_count": send_count, "hub_rows": hub_rows, "w_self": w_self, "w_neigh": w_neigh, "bias_term": bias_term, "cotangent": cotangent}


def silu_slope(pre_act):
    sigmoid_val = jax.nn.sigmoid(pre_act)
    return sigmoid_val * (1.0 + pre_act * (1.0 - sigmoid_val))


def reference(features, neighbours, degrees, send_rows, send_count, hub_rows, w_self, w_neigh, bias_term, cotangent):
    n_dev = N_ROW * N_COL
    feat_width = features.shape[1]
    tile_size = min(512, NODE_DEV)
    n_tiles = NODE_DEV // tile_size
    hub_owner = jnp.arange(n_dev * HUB_DEV, dtype=jnp.int32) // HUB_DEV
    hub_global = (hub_owner * NODE_DEV + hub_rows).astype(jnp.int32)
    all_hubs = features[hub_global]
    slot_index = jnp.arange(CAP, dtype=jnp.int32)
    source_ids = jnp.arange(n_dev, dtype=jnp.int32)
    table_len = NODE_DEV + n_dev * CAP + n_dev * HUB_DEV
    fan_index = jnp.arange(FANOUT, dtype=jnp.int32)

    def per_device(state_carry, device):
        grad_acc, self_acc, neigh_acc = state_carry
        base = (device * NODE_DEV).astype(jnp.int32)
        own_rows = lax.dynamic_slice_in_dim(features, base, NODE_DEV, 0)
        own_cot = lax.dynamic_slice_in_dim(cotangent, base, NODE_DEV, 0)
        own_nbrs = lax.dynamic_slice_in_dim(neighbours, base, NODE_DEV, 0)
        own_degs = lax.dynamic_slice_in_dim(degrees, base, NODE_DEV, 0)
        incoming_rows = lax.dynamic_slice_in_dim(send_rows, (device * CAP).astype(jnp.int32), CAP, 1)
        incoming_live = slot_index[None, :] < send_count[:, device][:, None]
        incoming_global = (source_ids[:, None] * NODE_DEV + incoming_rows).astype(jnp.int32)
        arrived = jnp.where(incoming_live[:, :, None], features[incoming_global], jnp.zeros((), features.dtype))
        arrived = arrived.reshape(n_dev * CAP, feat_width)
        src_table = jnp.concatenate([own_rows, arrived, all_hubs], 0)
        live_mask = fan_index[None, :] < own_degs[:, None]
        inv_deg = 1.0 / own_degs.astype(jnp.float32)

        def gather_tile(tile_index):
            tile_start = (tile_index * tile_size).astype(jnp.int32)
            tile_nbrs = lax.dynamic_slice_in_dim(own_nbrs, tile_start, tile_size, 0)
            tile_live = lax.dynamic_slice_in_dim(live_mask, tile_start, tile_size, 0)
            picked = src_table[tile_nbrs].astype(jnp.float32)
            return jnp.sum(jnp.where(tile_live[:, :, None], picked, 0.0), axis=1)

        summed = lax.map(gather_tile, jnp.arange(n_tiles, dtype=jnp.int32)).reshape(NODE_DEV, feat_width)
        aggregate = (summed * inv_deg[:, None]).astype(jnp.bfloat16)
        pre_act = (jnp.dot(own_rows, w_self, preferred_element_type=jnp.float32)
                   + jnp.dot(aggregate, w_neigh, preferred_element_type=jnp.float32)
                   + bias_term.astype(jnp.float32)[None, :])
        hidden = jax.nn.silu(pre_act).astype(jnp.bfloat16)
        d_pre = (own_cot.astype(jnp.float32) * silu_slope(pre_act)).astype(jnp.bfloat16)
        self_acc = self_acc + lax.dot_general(own_rows, d_pre, (((0,), (0,)), ((), ())), preferred_element_type=jnp.float32)
        neigh_acc = neigh_acc + lax.dot_general(aggregate, d_pre, (((0,), (0,)), ((), ())), preferred_element_type=jnp.float32)
        d_agg = lax.dot_general(d_pre, w_neigh, (((1,), (1,)), ((), ())), preferred_element_type=jnp.float32) * inv_deg[:, None]
        d_own = lax.dot_general(d_pre, w_self, (((1,), (1,)), ((), ())), preferred_element_type=jnp.float32)

        def spread_tile(tile_index, d_table):
            tile_start = (tile_index * tile_size).astype(jnp.int32)
            tile_nbrs = lax.dynamic_slice_in_dim(own_nbrs, tile_start, tile_size, 0)
            tile_live = lax.dynamic_slice_in_dim(live_mask, tile_start, tile_size, 0)
            tile_grad = lax.dynamic_slice_in_dim(d_agg, tile_start, tile_size, 0)
            target = jnp.where(tile_live, tile_nbrs, table_len).astype(jnp.int32)
            updates = jnp.broadcast_to(tile_grad[:, None, :], (tile_size, FANOUT, feat_width))
            return d_table.at[target.reshape(-1)].add(updates.reshape(-1, feat_width), mode="drop")

        d_table = lax.fori_loop(0, n_tiles, spread_tile, jnp.zeros((table_len, feat_width), jnp.float32))
        d_local = d_table[:NODE_DEV]
        d_arrived = d_table[NODE_DEV:NODE_DEV + n_dev * CAP]
        d_hubs = d_table[NODE_DEV + n_dev * CAP:]
        own_ids = (base + jnp.arange(NODE_DEV, dtype=jnp.int32)).astype(jnp.int32)
        grad_acc = grad_acc.at[own_ids].add(d_own + d_local)
        d_arrived = jnp.where(incoming_live.reshape(-1, 1), d_arrived, 0.0)
        grad_acc = grad_acc.at[incoming_global.reshape(-1)].add(d_arrived)
        grad_acc = grad_acc.at[hub_global].add(d_hubs)
        return (grad_acc, self_acc, neigh_acc), hidden

    init_state = (jnp.zeros((n_dev * NODE_DEV, feat_width), jnp.float32),
                  jnp.zeros((feat_width, feat_width), jnp.float32),
                  jnp.zeros((feat_width, feat_width), jnp.float32))
    final_state, hidden_all = lax.scan(per_device, init_state, jnp.arange(n_dev, dtype=jnp.int32))
    grad_acc, self_acc, neigh_acc = final_state
    return (hidden_all.reshape(n_dev * NODE_DEV, feat_width), grad_acc.astype(jnp.bfloat16),
            self_acc.astype(jnp.bfloat16), neigh_acc.astype(jnp.bfloat16))
```

```python
import jax
import jax.numpy as jnp
from jax import lax
from jax.sharding import PartitionSpec as P

AXES = ("row", "col")
BF16 = jnp.bfloat16
F32 = jnp.float32


def silu_slope(pre_act):
    sigmoid_val = jax.nn.sigmoid(pre_act)
    return sigmoid_val * (1.0 + pre_act * (1.0 - sigmoid_val))


def contract_rows(left, right):
    return lax.dot_general(left, right, (((0,), (0,)), ((), ())), preferred_element_type=F32)


def contract_cols(left, right):
    return lax.dot_general(left, right, (((1,), (1,)), ((), ())), preferred_element_type=F32)


def on_device(
    features,
    neighbours,
    degrees,
    send_rows,
    send_count,
    hub_rows,
    w_self,
    w_neigh,
    bias_term,
    cotangent,
):
    n_row = lax.axis_size("row")
    n_col = lax.axis_size("col")
    n_dev = n_row * n_col
    me = lax.axis_index("row") * n_col + lax.axis_index("col")
    n_local, width = features.shape
    fanout = neighbours.shape[1]
    n_slots = send_rows.shape[1]
    capacity = n_slots // n_dev
    n_hub = hub_rows.shape[0]
    half = width // 2

    core = n_col
    x_bits = [n_col << i for i in range(1, n_row.bit_length() - 1)]
    y_bits = [1]
    z_bits = [1 << i for i in range(1, n_col.bit_length() - 1)]

    def swap(value, mask):
        return lax.ppermute(value, AXES, [(i, i ^ mask) for i in range(n_dev)])

    def bit(mask):
        return (me & mask) // mask

    row_iota = jnp.arange(n_local, dtype=jnp.int32)
    slot_live = jnp.arange(capacity, dtype=jnp.int32)[None, :] < send_count.reshape(n_dev, 1)
    chosen = jnp.where(slot_live.reshape(-1), send_rows[0], -1)
    pick_send = (chosen[:, None] == row_iota[None, :]).astype(BF16)
    pick_hub = (hub_rows[:, None] == row_iota[None, :]).astype(BF16)
    own_hubs = jnp.dot(pick_hub, features, preferred_element_type=F32).astype(BF16)
    outgoing = jnp.dot(pick_send, features, preferred_element_type=F32).astype(BF16)
    arrived = lax.all_to_all(
        outgoing.reshape(n_dev, capacity, width), AXES, split_axis=0, concat_axis=0, tiled=True
    ).reshape(n_slots, width)

    hub_bits = z_bits + y_bits + x_bits + [core]
    hubs = own_hubs
    for mask in hub_bits:
        hubs = jnp.concatenate([hubs, swap(hubs, mask)], 0)
    peer_features = swap(features, core)

    hub_base = n_local + n_slots
    hub_id = neighbours - hub_base
    relative = (hub_id // n_hub) ^ me
    place = sum(((relative & mask) // mask) << i for i, mask in enumerate(hub_bits))
    where_to = jnp.where(hub_id >= 0, hub_base + place * n_hub + hub_id % n_hub, neighbours)
    where_to = jnp.where(jnp.arange(fanout, dtype=jnp.int32)[None, :] < degrees[:, None], where_to, -1)
    table_iota = jnp.arange(hub_base + n_dev * n_hub, dtype=jnp.int32)
    counts = sum((where_to[:, j : j + 1] == table_iota[None, :]).astype(F32) for j in range(fanout))
    counts = counts.astype(BF16)
    inv_deg = 1.0 / degrees.astype(F32)[:, None]

    summed = jnp.dot(counts[:, :n_local], features, preferred_element_type=F32)
    own_pre = jnp.dot(features, w_self, preferred_element_type=F32) + bias_term[None, :]
    summed = summed + jnp.dot(counts[:, n_local:hub_base], arrived, preferred_element_type=F32)
    summed = summed + jnp.dot(counts[:, hub_base:], hubs, preferred_element_type=F32)
    aggregate = (summed * inv_deg).astype(BF16)
    peer_aggregate = swap(aggregate, core)
    pre_act = own_pre + jnp.dot(aggregate, w_neigh, preferred_element_type=F32)
    hidden = jax.nn.silu(pre_act).astype(BF16)
    d_pre = (cotangent.astype(F32) * silu_slope(pre_act)).astype(BF16)

    d_agg = (contract_cols(d_pre, w_neigh) * inv_deg).astype(BF16)
    d_arrived = contract_rows(counts[:, n_local:hub_base], d_agg).astype(BF16)
    returned = lax.all_to_all(
        d_arrived.reshape(n_dev, capacity, width), AXES, split_axis=0, concat_axis=0, tiled=True
    ).reshape(n_slots, width)
    d_hubs = contract_rows(counts[:, hub_base:], d_agg)

    side = bit(core)
    mine = lax.dynamic_slice_in_dim(d_pre, side * half, half, 1)
    other = lax.dynamic_slice_in_dim(d_pre, (1 - side) * half, half, 1)
    peer_d_pre = swap(other, core)
    self_part = contract_rows(features, mine) + contract_rows(peer_features, peer_d_pre)
    neigh_part = contract_rows(aggregate, mine) + contract_rows(peer_aggregate, peer_d_pre)

    def keep_and_send(value, mask):
        size = value.shape[0] // 2
        b = bit(mask)
        keep = lax.dynamic_slice_in_dim(value, b * size, size, 0)
        send = lax.dynamic_slice_in_dim(value, (1 - b) * size, size, 0)
        return keep, send.astype(BF16)

    def fold_hubs(value):
        size = value.shape[0] // 2
        return value[:size], value[size:].astype(BF16)

    keep, send = fold_hubs(d_hubs)
    d_hubs = keep + swap(send, core).astype(F32)
    self_order = x_bits + y_bits
    neigh_order = y_bits + x_bits
    for self_mask, neigh_mask in zip(self_order, neigh_order):
        self_keep, self_send = keep_and_send(self_part, self_mask)
        neigh_keep, neigh_send = keep_and_send(neigh_part, neigh_mask)
        self_part = self_keep + swap(self_send, self_mask).astype(F32)
        neigh_part = neigh_keep + swap(neigh_send, neigh_mask).astype(F32)
    for mask in reversed(y_bits + x_bits):
        keep, send = fold_hubs(d_hubs)
        d_hubs = keep + swap(send, mask).astype(F32)

    n_z = 1 << len(z_bits)
    z_me = sum(bit(mask) << i for i, mask in enumerate(z_bits))
    piece = self_part.shape[0] // n_z
    total_self = lax.dynamic_slice_in_dim(self_part, z_me * piece, piece, 0)
    total_neigh = lax.dynamic_slice_in_dim(neigh_part, z_me * piece, piece, 0)
    hub_back = d_hubs[:n_hub]
    masks = [sum(mask for i, mask in enumerate(z_bits) if k >> i & 1) for k in range(n_z)]
    for k in range(1, n_z):
        to = z_me ^ k
        message = jnp.concatenate(
            [
                lax.dynamic_slice_in_dim(self_part, to * piece, piece, 0),
                lax.dynamic_slice_in_dim(neigh_part, to * piece, piece, 0),
                d_hubs[k * n_hub : (k + 1) * n_hub].reshape(2 * n_hub, half),
            ],
            0,
        ).astype(BF16)
        got = swap(message, masks[k]).astype(F32)
        total_self = total_self + got[:piece]
        total_neigh = total_neigh + got[piece : 2 * piece]
        hub_back = hub_back + got[2 * piece :].reshape(n_hub, width)

    own = jnp.stack([total_self, total_neigh]).astype(BF16)
    self_block = jnp.zeros((n_z * piece, half), BF16)
    neigh_block = jnp.zeros((n_z * piece, half), BF16)
    for k in range(n_z):
        got = own if k == 0 else swap(own, masks[k])
        at = (z_me ^ k) * piece
        self_block = lax.dynamic_update_slice_in_dim(self_block, got[0], at, 0)
        neigh_block = lax.dynamic_update_slice_in_dim(neigh_block, got[1], at, 0)

    def both(value, mask):
        got = swap(value, mask)
        b = bit(mask)
        return jnp.where(
            b == 0, jnp.concatenate([value, got], 0), jnp.concatenate([got, value], 0)
        )

    for self_mask, neigh_mask in zip(reversed(self_order), reversed(neigh_order)):
        self_block = both(self_block, self_mask)
        neigh_block = both(neigh_block, neigh_mask)

    def both_cols(value):
        got = swap(value, core)
        return jnp.where(
            side == 0, jnp.concatenate([value, got], 1), jnp.concatenate([got, value], 1)
        )

    grad_self = both_cols(self_block)
    grad_neigh = both_cols(neigh_block)

    d_local = contract_rows(counts[:, :n_local], d_agg)
    grad_x = contract_cols(d_pre, w_self) + d_local
    grad_x = grad_x + contract_rows(pick_send, returned)
    hub_high = hub_back.astype(BF16)
    hub_low = (hub_back - hub_high.astype(F32)).astype(BF16)
    grad_x = grad_x + contract_rows(
        jnp.concatenate([pick_hub, pick_hub], 0), jnp.concatenate([hub_high, hub_low], 0)
    )
    return hidden, grad_x.astype(BF16), grad_self, grad_neigh


def solution(mesh):
    split = P(AXES, None)
    in_specs = (split, split, P(AXES), split, split, P(AXES), P(), P(), P(), split)
    out_specs = (split, split, P(), P())
    return jax.shard_map(
        on_device, mesh=mesh, in_specs=in_specs, out_specs=out_specs, check_vma=False
    )
```

```python
import functools

import jax
import jax.numpy as jnp
from jax import lax
from jax.experimental import pallas as pl
from jax.experimental.pallas import tpu as pltpu
from jax.sharding import PartitionSpec as P

AXES = ("row", "col")
BF16 = jnp.bfloat16
F32 = jnp.float32
CHUNK = 256
HBM = pl.BlockSpec(memory_space=pl.ANY)
VMEM_LIMIT = 56 << 20
SMEM = pl.BlockSpec(memory_space=pltpu.SMEM)


def mul(left, right):
    return jnp.dot(left, right, preferred_element_type=F32)


def mul_t(left, right):
    return lax.dot_general(left, right, (((1,), (1,)), ((), ())), preferred_element_type=F32)


def t_mul(left, right):
    return lax.dot_general(left, right, (((0,), (0,)), ((), ())), preferred_element_type=F32)


def run(body, scalars, ins, outs, flops=0, scratch=()):
    n_in, n_out = len(ins), len(outs)
    outs = [jax.ShapeDtypeStruct(shape, dtype) for shape, dtype in outs]

    def kernel(*refs):
        scalar_ref, refs = refs[0], refs[1:]
        in_hbm, out_hbm = refs[:n_in], refs[n_in : n_in + n_out]
        refs = refs[n_in + n_out :]
        in_buf, out_buf = refs[:n_in], refs[n_in : n_in + n_out]
        extra, (in_sem, out_sem) = refs[n_in + n_out : -2], refs[-2:]
        loads = [pltpu.make_async_copy(in_hbm[i], in_buf[i], in_sem.at[i]) for i in range(n_in)]
        stores = [pltpu.make_async_copy(out_buf[i], out_hbm[i], out_sem.at[i]) for i in range(n_out)]
        for load in loads:
            load.start()

        def need(*which):
            for i in which:
                loads[i].wait()

        def emit(*which):
            for i in which:
                stores[i].start()

        body(scalar_ref, in_buf, out_buf, need, emit, *extra)
        for store in stores:
            store.wait()

    held = sum(a.size * a.dtype.itemsize for a in [*ins, *outs])
    return pl.pallas_call(
        kernel,
        out_shape=outs,
        in_specs=[SMEM] + [HBM] * n_in,
        out_specs=[HBM] * n_out,
        scratch_shapes=[pltpu.VMEM(a.shape, a.dtype) for a in [*ins, *outs]]
        + list(scratch)
        + [pltpu.SemaphoreType.DMA((n_in,)), pltpu.SemaphoreType.DMA((n_out,))],
        compiler_params=pltpu.CompilerParams(vmem_limit_bytes=VMEM_LIMIT),
        cost_estimate=pl.CostEstimate(flops=flops, bytes_accessed=held, transcendentals=0),
    )(scalars, *ins)


def one_hot(ids, n_local):
    rows = lax.broadcasted_iota(jnp.int32, (n_local, ids.shape[1]), 0)
    return (rows == ids).astype(F32).astype(BF16)


def pack_body(scalars, ins, outs, need, emit):
    features, send_rows, send_count, hub_rows = ins
    outgoing, own_hubs, chosen = outs
    n_local = features.shape[0]
    n_slots, n_dev = send_rows.shape[1], send_count.shape[1]
    capacity = n_slots // n_dev
    need(1, 2, 3)
    peer = lax.broadcasted_iota(jnp.int32, (n_dev, n_slots), 0)
    lane = lax.broadcasted_iota(jnp.int32, (n_dev, n_slots), 1)
    spread = (lane // capacity == peer).astype(F32)
    live = mul(send_count[...].astype(F32), spread)
    slot = lax.broadcasted_iota(jnp.int32, (1, n_slots), 1) % capacity
    ids = jnp.where(slot.astype(F32) < live, send_rows[...], -1)
    chosen[...] = ids
    emit(2)
    pick = one_hot(ids, n_local)
    pick_hub = one_hot(hub_rows[...], n_local)
    need(0)
    own_hubs[...] = t_mul(pick_hub, features[...]).astype(BF16)
    emit(1)
    outgoing[...] = t_mul(pick, features[...]).astype(BF16)
    emit(0)


def seed_body(side, ins, outs, need, emit, d_pre_all, aggregate):
    counts, arrived, hubs, summed, inv_deg, w_neigh, own_pre, cotangent, counts_t = ins
    hidden, d_pre, d_agg, d_pre_other, aggregate_t, d_arrived, hub_keep, hub_send = outs
    n_local, width = cotangent.shape
    n_slots = arrived.shape[0]
    n_hubs = hubs.shape[0]
    half = width // 2
    need(0, 1, 2, 3, 4)
    inv = inv_deg[...]
    for c in range(0, width, CHUNK):
        cols = slice(c, c + CHUNK)
        total = summed[:, cols] + mul(counts[:, :n_slots], arrived[:, cols])
        total = total + mul(counts[:, n_slots:], hubs[:, cols])
        mean = total * inv
        aggregate[:, cols] = mean.astype(BF16)
        aggregate_t[cols, :] = mean.T.astype(BF16)
    emit(4)
    need(5, 6, 7)
    for c in range(0, width, CHUNK):
        cols = slice(c, c + CHUNK)
        pre = own_pre[:, cols] + mul(aggregate[...], w_neigh[:, cols])
        sig = 0.5 + 0.5 * jnp.tanh(0.5 * pre)
        hidden[:, cols] = (pre * sig).astype(BF16)
        grad = cotangent[:, cols].astype(F32) * (sig * (1.0 + pre * (1.0 - sig)))
        grad = grad.astype(BF16)
        d_pre_all[:, cols] = grad
        part = slice(c % half, c % half + CHUNK)

        @pl.when(side[0] == c // half)
        def _():
            d_pre[:, part] = grad

        @pl.when(side[0] != c // half)
        def _():
            d_pre_other[:, part] = grad

    emit(3, 1, 0)
    need(8)
    for c in range(0, width, CHUNK):
        cols = slice(c, c + CHUNK)
        grad = (mul_t(d_pre_all[...], w_neigh[cols, :]) * inv).astype(BF16)
        d_agg[:, cols] = grad
        d_arrived[:, cols] = mul(counts_t[:n_slots, :], grad).astype(BF16)
        d_hubs = mul(counts_t[n_slots:, :], grad)
        part = slice(c % half, c % half + CHUNK)
        hub_keep[c // half, :, part] = d_hubs[: n_hubs // 2]
        hub_send[c // half, :, part] = d_hubs[n_hubs // 2 :].astype(BF16)
    emit(5, 7, 6, 2)


def hub_rows_of(total, k, rows):
    return jnp.concatenate([total[0, k * rows : (k + 1) * rows], total[1, k * rows : (k + 1) * rows]], 0)


def weight_body(n_part, with_hubs, mine, ins, outs, need, emit):
    own, peer, d_own, d_peer = ins[:4]
    rows, half = outs[0].shape
    need(*range(len(ins)))
    for k in [*range(1, n_part), 0]:
        at = pl.multiple_of((mine[0] ^ k) * rows, rows)
        for r in range(0, rows, min(rows, CHUNK)):
            block = pl.ds(at + r, min(rows, CHUNK))
            total = mul(own[block, :], d_own[...]) + mul(peer[block, :], d_peer[...])
            outs[k][r : r + min(rows, CHUNK), :] = total.astype(outs[k].dtype)
        if k > 0 and with_hubs:
            hubs = ins[4][...] + ins[5][...].astype(F32)
            size = hubs.shape[1] // n_part
            outs[k][rows:, :] = hub_rows_of(hubs, k, size).astype(BF16)
        if k > 0:
            emit(k)
    if with_hubs:
        size = ins[4].shape[1] // n_part
        outs[n_part][...] = ins[4][:, :size] + ins[5][:, :size].astype(F32)
        emit(n_part)
    emit(0)


def fold_body(n_part, n_got, mine, ins, outs, need, emit, total):
    self_keep, neigh_keep, hubs = ins[:3]
    self_got, neigh_got = ins[3 : 3 + n_got], ins[3 + n_got :]
    size = self_keep.shape[0]
    rows = size // n_part
    n_hub = hubs.shape[1]
    need(*range(len(ins)))
    together = len(neigh_got) == 0
    self_value, neigh_value = self_keep[...], neigh_keep[...]
    first, second = hubs[0], hubs[1]
    for i in range(n_got):
        self_value = self_value + self_got[i][:size, :].astype(F32)
        if together:
            neigh_value = neigh_value + self_got[i][size : 2 * size, :].astype(F32)
            tail = self_got[i][2 * size :, :].astype(F32)
        else:
            neigh_value = neigh_value + neigh_got[i][...].astype(F32)
            tail = self_got[i][size:, :].astype(F32)
        first = first + tail[:n_hub]
        second = second + tail[n_hub:]
    if n_part == 1:
        outs[0][:size, :] = self_value.astype(BF16)
        outs[0][size:, :] = neigh_value.astype(BF16)
        outs[1][0] = first
        outs[1][1] = second
        emit(0, 1)
        return
    n_hub = n_hub // n_part
    total[0] = self_value
    total[1] = neigh_value
    for k in [*range(1, n_part), 0]:
        at = pl.ds(pl.multiple_of((mine[0] ^ k) * rows, rows), rows)
        span = slice(k * n_hub, (k + 1) * n_hub)
        if k > 0:
            outs[k + 2][:rows, :] = total[0, at, :].astype(BF16)
            outs[k + 2][rows : 2 * rows, :] = total[1, at, :].astype(BF16)
            outs[k + 2][2 * rows :, :] = jnp.concatenate([first[span], second[span]], 0).astype(BF16)
            emit(k + 2)
    at = pl.ds(pl.multiple_of(mine[0] * rows, rows), rows)
    outs[0][...] = total[0, at, :]
    outs[1][...] = total[1, at, :]
    outs[2][0] = first[:n_hub]
    outs[2][1] = second[:n_hub]
    emit(0, 1, 2)


def node_body(side, ins, outs, need, emit):
    w_self, d_pre, d_other, counts_t, d_agg, chosen, returned, hub_rows, hub_back = ins
    (grad_x,) = outs
    n_local = d_pre.shape[0]
    width = w_self.shape[0]
    half = width // 2
    need(*range(len(ins)))
    picked = one_hot(chosen[...], n_local)
    hub_picked = one_hot(hub_rows[...], n_local)
    mine = pl.ds(pl.multiple_of(side[0] * half, half), half)
    theirs = pl.ds(pl.multiple_of((1 - side[0]) * half, half), half)
    for c in range(0, width, CHUNK):
        cols = slice(c, c + CHUNK)
        part = slice(c % half, c % half + CHUNK)
        back = hub_back[c // half, :, part]
        high = back.astype(BF16)
        low = (back - high.astype(F32)).astype(BF16)
        total = mul_t(d_pre[...], w_self[cols, mine]) + mul_t(d_other[...], w_self[cols, theirs])
        total = total + mul(counts_t[...], d_agg[:, cols])
        total = total + mul(picked, returned[:, cols])
        total = total + mul(hub_picked, high) + mul(hub_picked, low)
        grad_x[:, cols] = total.astype(BF16)
    emit(0)


def place_body(n_xy, n_z, where, ins, outs, need, emit):
    size, half = ins[0].shape
    size = size // 2
    rows = size // n_z
    for i in range(2 * n_xy):
        core, k = divmod(i, n_xy)
        need(i)
        cols = pl.ds(pl.multiple_of((where[0] ^ core) * half, half), half)
        for grad in range(2):
            for j in range(n_z):
                at = (where[1] ^ k) * size + (where[2] ^ j) * rows
                piece = ins[i][(2 * j + grad) * rows : (2 * j + grad + 1) * rows, :]
                outs[grad][pl.ds(pl.multiple_of(at, rows), rows), cols] = piece
    emit(0, 1)


def on_device(
    features,
    neighbours,
    degrees,
    send_rows,
    send_count,
    hub_rows,
    w_self,
    w_neigh,
    bias_term,
    cotangent,
):
    n_row = lax.axis_size("row")
    n_col = lax.axis_size("col")
    n_dev = n_row * n_col
    me = lax.axis_index("row") * n_col + lax.axis_index("col")
    n_local, width = features.shape
    fanout = neighbours.shape[1]
    n_slots = send_rows.shape[1]
    capacity = n_slots // n_dev
    n_hub = hub_rows.shape[0]
    n_hubs = n_dev * n_hub
    half = width // 2
    hub_base = n_local + n_slots
    wide = (n_local, width)

    core = n_col
    xy_bits = [1] + [n_col << i for i in range(1, n_row.bit_length() - 1)]
    z_bits = [1 << i for i in range(1, n_col.bit_length() - 1)]
    hub_bits = z_bits + xy_bits + [core]
    n_xy, n_z = 1 << len(xy_bits), 1 << len(z_bits)

    def spread(bits, k):
        return sum(mask for i, mask in enumerate(bits) if k >> i & 1)

    def bit(mask):
        return (me & mask) // mask

    def place_of(bits):
        return sum(bit(mask) << i for i, mask in enumerate(bits))

    def swap(value, mask):
        return lax.ppermute(value, AXES, [(i, i ^ mask) for i in range(n_dev)])

    side, xy_me, z_me = bit(core), place_of(xy_bits), place_of(z_bits)

    hub_row = hub_rows.reshape(1, n_hub)
    outgoing, own_hubs, chosen = run(
        pack_body,
        side[None],
        [features, send_rows, send_count, hub_row],
        [((n_slots, width), BF16), ((n_hub, width), BF16), ((1, n_slots), jnp.int32)],
        flops=2 * n_slots * n_local * width,
    )
    arrived = lax.all_to_all(
        outgoing.reshape(n_dev, capacity, width), AXES, split_axis=0, concat_axis=0, tiled=True
    ).reshape(n_slots, width)

    hubs = jnp.concatenate([own_hubs] + [swap(own_hubs, spread(z_bits, k)) for k in range(1, n_z)], 0)
    for mask in xy_bits + [core]:
        hubs = jnp.concatenate([hubs, swap(hubs, mask)], 0)
    feat_t = features.T
    peer_feat_t = swap(feat_t, core)

    hub_id = neighbours - hub_base
    relative = (hub_id // n_hub) ^ me
    spot = sum(((relative & mask) // mask) << i for i, mask in enumerate(hub_bits))
    where_to = jnp.where(hub_id >= 0, hub_base + spot * n_hub + hub_id % n_hub, neighbours)
    where_to = jnp.where(jnp.arange(fanout, dtype=jnp.int32)[None, :] < degrees[:, None], where_to, -1)
    to_t = where_to.T

    def count(first, last):
        ids = jnp.arange(first, last, dtype=jnp.int32)
        found = sum((where_to[:, j : j + 1] == ids[None, :]).astype(F32) for j in range(fanout))
        found_t = sum((to_t[j : j + 1, :] == ids[:, None]).astype(F32) for j in range(fanout))
        return found.astype(BF16), found_t.astype(BF16)

    counts_own, counts_own_t = count(0, n_local)
    counts_far, counts_far_t = count(n_local, hub_base + n_hubs)
    inv_deg = 1.0 / degrees.astype(F32)[:, None]
    summed = mul(counts_own, features)
    own_pre = mul(features, w_self) + bias_term[None, :]

    hidden, d_pre, d_agg, d_other, agg_t, d_arrived, hub_keep, hub_send = run(
        seed_body,
        side[None],
        [counts_far, arrived, hubs, summed, inv_deg, w_neigh, own_pre, cotangent, counts_far_t],
        [
            (wide, BF16),
            ((n_local, half), BF16),
            (wide, BF16),
            ((n_local, half), BF16),
            ((width, n_local), BF16),
            ((n_slots, width), BF16),
            ((2, n_hubs // 2, half), F32),
            ((2, n_hubs // 2, half), BF16),
        ],
        flops=4 * n_local * width * (width + n_slots + n_hubs),
        scratch=[pltpu.VMEM(wide, BF16), pltpu.VMEM(wide, BF16)],
    )
    returned = lax.all_to_all(
        d_arrived.reshape(n_dev, capacity, width), AXES, split_axis=0, concat_axis=0, tiled=True
    ).reshape(n_slots, width)
    peer_d_pre = swap(d_other, core)
    hub_got = swap(hub_send, core)
    peer_agg_t = swap(agg_t, core)

    xy_rows, z_rows = width // n_xy, width // n_xy // n_z
    hub_xy, hub_z = n_hubs // 2 // n_xy, n_hubs // 2 // n_xy // n_z

    def reduce_start(own, peer, with_hubs):
        extra = 2 * hub_xy if with_hubs else 0
        outs = [((xy_rows, half), F32)] + [((xy_rows + extra, half), BF16)] * (n_xy - 1)
        hub_in = [hub_keep, hub_got] if with_hubs else []
        hub_out = [((2, hub_xy, half), F32)] if with_hubs else []
        return run(
            functools.partial(weight_body, n_xy, with_hubs),
            xy_me[None],
            [own, peer, d_pre, peer_d_pre] + hub_in,
            outs + hub_out,
            flops=4 * width * half * n_local,
        )

    def across(parts, bits):
        return [swap(part, spread(bits, k + 1)) for k, part in enumerate(parts)]

    self_parts = reduce_start(feat_t, peer_feat_t, True)
    self_got = across(self_parts[1:n_xy], xy_bits)
    neigh_parts = reduce_start(agg_t, peer_agg_t, False)
    neigh_got = across(neigh_parts[1:n_xy], xy_bits)
    parts = run(
        functools.partial(fold_body, n_z, n_xy - 1),
        z_me[None],
        [self_parts[0], neigh_parts[0], self_parts[n_xy]] + self_got + neigh_got,
        [((z_rows, half), F32)] * 2
        + [((2, hub_z, half), F32)]
        + [((2 * z_rows + 2 * hub_z, half), BF16)] * (n_z - 1),
        scratch=[pltpu.VMEM((2, xy_rows, half), F32)],
    )
    own, hub_back = run(
        functools.partial(fold_body, 1, n_z - 1),
        z_me[None],
        list(parts[:3]) + across(parts[3:], z_bits),
        [((2 * z_rows, half), BF16), ((2, hub_z, half), F32)],
        scratch=[pltpu.VMEM((2, 8, half), F32)],
    )
    line = jnp.concatenate([own] + across([own] * (n_z - 1), z_bits), 0)
    line, returned = lax.optimization_barrier((line, returned))
    blocks = [line] + across([line] * (n_xy - 1), xy_bits)
    blocks = blocks + [swap(one, core) for one in blocks]
    grad_self, grad_neigh = run(
        functools.partial(place_body, n_xy, n_z),
        jnp.stack([side, xy_me, z_me]),
        blocks,
        [((width, width), BF16)] * 2,
    )
    (grad_x,) = run(
        node_body,
        side[None],
        [w_self, d_pre, d_other, counts_own_t, d_agg, chosen, returned, hub_row, hub_back],
        [(wide, BF16)],
        flops=2 * n_local * width * (width + n_local + n_slots),
    )
    return hidden, grad_x, grad_self, grad_neigh


def solution(mesh):
    split = P(AXES, None)
    in_specs = (split, split, P(AXES), split, split, P(AXES), P(), P(), P(), split)
    out_specs = (split, split, P(), P())
    return jax.shard_map(
        on_device, mesh=mesh, in_specs=in_specs, out_specs=out_specs, check_vma=False
    )
```

```python
import functools

import jax
import jax.numpy as jnp
from jax import lax
from jax.experimental import pallas as pl
from jax.experimental.pallas import tpu as pltpu
from jax.sharding import PartitionSpec as P

AXES = ("row", "col")
BF16 = jnp.bfloat16
F32 = jnp.float32
CHUNK = 512
HBM = pl.BlockSpec(memory_space=pl.ANY)
VMEM_LIMIT = 56 << 20
VMEM = pl.BlockSpec(memory_space=pltpu.VMEM)
SMEM = pl.BlockSpec(memory_space=pltpu.SMEM)


def mul(left, right):
    return jnp.dot(left, right, preferred_element_type=F32)


def mul_t(left, right):
    return lax.dot_general(left, right, (((1,), (1,)), ((), ())), preferred_element_type=F32)


def t_mul(left, right):
    return lax.dot_general(left, right, (((0,), (0,)), ((), ())), preferred_element_type=F32)


def run(body, scalars, ins, outs, flops=0, scratch=(), limit=0):
    n_in, n_out = len(ins), len(outs)
    outs = [jax.ShapeDtypeStruct(shape, dtype) for shape, dtype in outs]

    def kernel(*refs):
        scalar_ref, refs = refs[0], refs[1:]
        in_hbm, out_hbm = refs[:n_in], refs[n_in : n_in + n_out]
        refs = refs[n_in + n_out :]
        in_buf, out_buf = refs[:n_in], refs[n_in : n_in + n_out]
        extra, (in_sem, out_sem) = refs[n_in + n_out : -2], refs[-2:]
        loads = [pltpu.make_async_copy(in_hbm[i], in_buf[i], in_sem.at[i]) for i in range(n_in)]
        stores = [pltpu.make_async_copy(out_buf[i], out_hbm[i], out_sem.at[i]) for i in range(n_out)]
        for load in loads:
            load.start()

        def need(*which):
            for i in which:
                loads[i].wait()

        def emit(*which):
            for i in which:
                stores[i].start()

        body(scalar_ref, in_buf, out_buf, need, emit, *extra)
        for store in stores:
            store.wait()

    held = sum(a.size * a.dtype.itemsize for a in [*ins, *outs])
    return pl.pallas_call(
        kernel,
        out_shape=outs,
        in_specs=[SMEM] + [HBM] * n_in,
        out_specs=[HBM] * n_out,
        scratch_shapes=[pltpu.VMEM(a.shape, a.dtype) for a in [*ins, *outs]]
        + list(scratch)
        + [pltpu.SemaphoreType.DMA((n_in,)), pltpu.SemaphoreType.DMA((n_out,))],
        compiler_params=pltpu.CompilerParams(vmem_limit_bytes=limit or held + (8 << 20)),
        cost_estimate=pl.CostEstimate(flops=flops, bytes_accessed=held, transcendentals=0),
    )(scalars, *ins)


def run_inside(body, scalars, ins, outs, flops=0, scratch=()):
    n_in, n_out = len(ins), len(outs)
    outs = [jax.ShapeDtypeStruct(shape, dtype) for shape, dtype in outs]

    def kernel(*refs):
        body(refs[0], refs[1 : 1 + n_in], refs[1 + n_in : 1 + n_in + n_out], *refs[1 + n_in + n_out :])

    held = sum(a.size * a.dtype.itemsize for a in [*ins, *outs])
    return pl.pallas_call(
        kernel,
        out_shape=outs,
        in_specs=[SMEM] + [VMEM] * n_in,
        out_specs=[VMEM] * n_out,
        scratch_shapes=list(scratch),
        compiler_params=pltpu.CompilerParams(vmem_limit_bytes=held + (8 << 20)),
        cost_estimate=pl.CostEstimate(flops=flops, bytes_accessed=held, transcendentals=0),
    )(scalars, *ins)


def one_hot(ids, n_local):
    rows = lax.broadcasted_iota(jnp.int32, (n_local, ids.shape[1]), 0)
    return (rows == ids).astype(F32).astype(BF16)


def pack_body(scalars, ins, outs, need, emit):
    features, send_rows, send_count, hub_rows = ins
    outgoing, own_hubs, chosen = outs
    n_local = features.shape[0]
    n_slots, n_dev = send_rows.shape[1], send_count.shape[1]
    capacity = n_slots // n_dev
    need(1, 2, 3)
    peer = lax.broadcasted_iota(jnp.int32, (n_dev, n_slots), 0)
    lane = lax.broadcasted_iota(jnp.int32, (n_dev, n_slots), 1)
    spread = (lane // capacity == peer).astype(F32)
    live = mul(send_count[...].astype(F32), spread)
    slot = lax.broadcasted_iota(jnp.int32, (1, n_slots), 1) % capacity
    ids = jnp.where(slot.astype(F32) < live, send_rows[...], -1)
    chosen[...] = ids
    emit(2)
    pick = one_hot(ids, n_local)
    pick_hub = one_hot(hub_rows[...], n_local)
    need(0)
    own_hubs[...] = t_mul(pick_hub, features[...]).astype(BF16)
    emit(1)
    outgoing[...] = t_mul(pick, features[...]).astype(BF16)
    emit(0)


def seed_body(side, ins, outs, need, emit, d_pre_all, aggregate):
    counts, arrived, hubs, summed, inv_deg, w_neigh, own_pre, cotangent, counts_t = ins
    hidden, d_pre, d_agg, d_pre_other, aggregate_t, d_arrived, hub_keep, hub_send = outs
    n_local, width = cotangent.shape
    n_slots = arrived.shape[0]
    n_hubs = hubs.shape[0]
    half = width // 2
    need(0, 1, 2, 3, 4)
    inv = inv_deg[...]
    for c in range(0, width, CHUNK):
        cols = slice(c, c + CHUNK)
        total = summed[:, cols] + mul(counts[:, :n_slots], arrived[:, cols])
        total = total + mul(counts[:, n_slots:], hubs[:, cols])
        mean = total * inv
        aggregate[:, cols] = mean.astype(BF16)
        aggregate_t[cols, :] = mean.T.astype(BF16)
    emit(4)
    need(5, 6, 7)
    for c in range(0, width, CHUNK):
        cols = slice(c, c + CHUNK)
        pre = own_pre[:, cols] + mul(aggregate[...], w_neigh[:, cols])
        sig = 0.5 + 0.5 * jnp.tanh(0.5 * pre)
        hidden[:, cols] = (pre * sig).astype(BF16)
        grad = cotangent[:, cols].astype(F32) * (sig * (1.0 + pre * (1.0 - sig)))
        grad = grad.astype(BF16)
        d_pre_all[:, cols] = grad
        part = slice(c % half, c % half + CHUNK)

        @pl.when(side[0] == c // half)
        def _():
            d_pre[:, part] = grad

        @pl.when(side[0] != c // half)
        def _():
            d_pre_other[:, part] = grad

    emit(3, 1, 0)
    need(8)
    for c in range(0, width, CHUNK):
        cols = slice(c, c + CHUNK)
        grad = (mul_t(d_pre_all[...], w_neigh[cols, :]) * inv).astype(BF16)
        d_agg[:, cols] = grad
        d_arrived[:, cols] = mul(counts_t[:n_slots, :], grad).astype(BF16)
        d_hubs = mul(counts_t[n_slots:, :], grad)
        part = slice(c % half, c % half + CHUNK)
        hub_keep[c // half, :, part] = d_hubs[: n_hubs // 2]
        hub_send[c // half, :, part] = d_hubs[n_hubs // 2 :].astype(BF16)
    emit(5, 7, 6, 2)


def hub_rows_of(total, k, rows):
    return jnp.concatenate([total[0, k * rows : (k + 1) * rows], total[1, k * rows : (k + 1) * rows]], 0)


def weight_body(n_part, with_hubs, mine, ins, outs, total):
    own, peer, d_own, d_peer = ins[:4]
    rows, half = outs[0].shape
    total[...] = mul(own[...], d_own[...]) + mul(peer[...], d_peer[...])
    if with_hubs:
        hubs = ins[4][...] + ins[5][...].astype(F32)
        size = hubs.shape[1] // n_part
        outs[n_part][...] = hubs[:, :size]
    for k in range(n_part):
        at = pl.ds(pl.multiple_of((mine[0] ^ k) * rows, rows), rows)
        outs[k][:rows, :] = total[at, :].astype(outs[k].dtype)
        if k > 0 and with_hubs:
            outs[k][rows:, :] = hub_rows_of(hubs, k, size).astype(BF16)


def add_up(keep, hubs, got):
    size = keep.shape[0]
    value = keep[...]
    for one in got:
        value = value + one[:size, :].astype(F32)
    if hubs is None:
        return value, None, None
    first, second = hubs[0], hubs[1]
    n_hub = first.shape[0]
    for one in got:
        tail = one[size:, :].astype(F32)
        first = first + tail[:n_hub]
        second = second + tail[n_hub:]
    return value, first, second


def fold_body(n_part, with_hubs, mine, ins, outs, total):
    hubs = ins[1] if with_hubs else None
    rows = outs[0].shape[0]
    value, first, second = add_up(ins[0], hubs, ins[1 + int(with_hubs) :])
    total[...] = value
    if with_hubs:
        n_hub = first.shape[0] // n_part
        outs[n_part][0] = first[:n_hub]
        outs[n_part][1] = second[:n_hub]
    for k in range(n_part):
        at = pl.ds(pl.multiple_of((mine[0] ^ k) * rows, rows), rows)
        outs[k][:rows, :] = total[at, :].astype(outs[k].dtype)
        if k > 0 and with_hubs:
            span = slice(k * n_hub, (k + 1) * n_hub)
            outs[k][rows:, :] = jnp.concatenate([first[span], second[span]], 0).astype(BF16)


def last_body(n_got, scalars, ins, outs):
    own, hub_back = outs
    rows = ins[0].shape[0]
    value, _, _ = add_up(ins[0], None, ins[3 : 3 + n_got])
    own[:rows, :] = value.astype(BF16)
    value, first, second = add_up(ins[1], ins[2], ins[3 + n_got :])
    own[rows:, :] = value.astype(BF16)
    hub_back[0] = first
    hub_back[1] = second


def join_body(scalars, ins, outs):
    at = 0
    for one in ins:
        outs[0][at : at + one.shape[0], :] = one[...]
        at += one.shape[0]


def node_body(side, ins, outs, need, emit):
    w_self, d_pre, d_other, counts_t, d_agg, chosen, returned, hub_rows, hub_back = ins
    (grad_x,) = outs
    n_local = d_pre.shape[0]
    width = w_self.shape[0]
    half = width // 2
    need(*range(len(ins)))
    picked = one_hot(chosen[...], n_local)
    hub_picked = one_hot(hub_rows[...], n_local)
    mine = pl.ds(pl.multiple_of(side[0] * half, half), half)
    theirs = pl.ds(pl.multiple_of((1 - side[0]) * half, half), half)
    for c in range(0, width, CHUNK):
        cols = slice(c, c + CHUNK)
        part = slice(c % half, c % half + CHUNK)
        back = hub_back[c // half, :, part]
        high = back.astype(BF16)
        low = (back - high.astype(F32)).astype(BF16)
        total = mul_t(d_pre[...], w_self[cols, mine]) + mul_t(d_other[...], w_self[cols, theirs])
        total = total + mul(counts_t[...], d_agg[:, cols])
        total = total + mul(picked, returned[:, cols])
        total = total + mul(hub_picked, high) + mul(hub_picked, low)
        grad_x[:, cols] = total.astype(BF16)
    emit(0)


def place_body(n_xy, n_z, n_share, where, ins, outs):
    half = ins[0].shape[1]
    n_piece = n_z // n_share
    rows = ins[0].shape[0] // n_piece // 2
    for i, block in enumerate(ins):
        core, share, k = i // (n_share * n_xy), i // n_xy % n_share, i % n_xy
        cols = pl.ds(pl.multiple_of((where[0] ^ core) * half, half), half)
        for j in range(n_piece):
            z = where[2] ^ (share * n_piece + j)
            at = pl.ds(pl.multiple_of(((where[1] ^ k) * n_z + z) * rows, rows), rows)
            for grad in range(2):
                first = (2 * j + grad) * rows
                outs[grad][at, cols] = block[first : first + rows, :]


def on_device(
    features,
    neighbours,
    degrees,
    send_rows,
    send_count,
    hub_rows,
    w_self,
    w_neigh,
    bias_term,
    cotangent,
):
    n_row = lax.axis_size("row")
    n_col = lax.axis_size("col")
    n_dev = n_row * n_col
    me = lax.axis_index("row") * n_col + lax.axis_index("col")
    n_local, width = features.shape
    fanout = neighbours.shape[1]
    n_slots = send_rows.shape[1]
    capacity = n_slots // n_dev
    n_hub = hub_rows.shape[0]
    n_hubs = n_dev * n_hub
    half = width // 2
    hub_base = n_local + n_slots
    wide = (n_local, width)

    core = n_col
    xy_bits = [1] + [n_col << i for i in range(1, n_row.bit_length() - 1)]
    z_bits = [1 << i for i in range(1, n_col.bit_length() - 1)]
    hub_bits = z_bits + xy_bits + [core]
    n_xy, n_z = 1 << len(xy_bits), 1 << len(z_bits)

    def spread(bits, k):
        return sum(mask for i, mask in enumerate(bits) if k >> i & 1)

    def bit(mask):
        return (me & mask) // mask

    def place_of(bits):
        return sum(bit(mask) << i for i, mask in enumerate(bits))

    def swap(value, mask):
        return lax.ppermute(value, AXES, [(i, i ^ mask) for i in range(n_dev)])

    side, xy_me, z_me = bit(core), place_of(xy_bits), place_of(z_bits)

    hub_row = hub_rows.reshape(1, n_hub)
    outgoing, own_hubs, chosen = run(
        pack_body,
        side[None],
        [features, send_rows, send_count, hub_row],
        [((n_slots, width), BF16), ((n_hub, width), BF16), ((1, n_slots), jnp.int32)],
        flops=2 * n_slots * n_local * width,
        limit=VMEM_LIMIT,
    )
    arrived = lax.all_to_all(
        outgoing.reshape(n_dev, capacity, width), AXES, split_axis=0, concat_axis=0, tiled=True
    ).reshape(n_slots, width)

    hubs = jnp.concatenate([own_hubs] + [swap(own_hubs, spread(z_bits, k)) for k in range(1, n_z)], 0)
    for mask in xy_bits + [core]:
        hubs = jnp.concatenate([hubs, swap(hubs, mask)], 0)
    feat_t = features.T
    peer_feat_t = swap(feat_t, core)

    hub_id = neighbours - hub_base
    relative = (hub_id // n_hub) ^ me
    spot = sum(((relative & mask) // mask) << i for i, mask in enumerate(hub_bits))
    where_to = jnp.where(hub_id >= 0, hub_base + spot * n_hub + hub_id % n_hub, neighbours)
    where_to = jnp.where(jnp.arange(fanout, dtype=jnp.int32)[None, :] < degrees[:, None], where_to, -1)
    to_t = where_to.T

    def count(first, last):
        ids = jnp.arange(first, last, dtype=jnp.int32)
        found = sum((where_to[:, j : j + 1] == ids[None, :]).astype(F32) for j in range(fanout))
        found_t = sum((to_t[j : j + 1, :] == ids[:, None]).astype(F32) for j in range(fanout))
        return found.astype(BF16), found_t.astype(BF16)

    counts_own, counts_own_t = count(0, n_local)
    counts_far, counts_far_t = count(n_local, hub_base + n_hubs)
    inv_deg = 1.0 / degrees.astype(F32)[:, None]
    summed = mul(counts_own, features)
    own_pre = mul(features, w_self) + bias_term[None, :]

    hidden, d_pre, d_agg, d_other, agg_t, d_arrived, hub_keep, hub_send = run(
        seed_body,
        side[None],
        [counts_far, arrived, hubs, summed, inv_deg, w_neigh, own_pre, cotangent, counts_far_t],
        [
            (wide, BF16),
            ((n_local, half), BF16),
            (wide, BF16),
            ((n_local, half), BF16),
            ((width, n_local), BF16),
            ((n_slots, width), BF16),
            ((2, n_hubs // 2, half), F32),
            ((2, n_hubs // 2, half), BF16),
        ],
        flops=4 * n_local * width * (width + n_slots + n_hubs),
        scratch=[pltpu.VMEM(wide, BF16), pltpu.VMEM(wide, BF16)],
        limit=VMEM_LIMIT,
    )
    returned = lax.all_to_all(
        d_arrived.reshape(n_dev, capacity, width), AXES, split_axis=0, concat_axis=0, tiled=True
    ).reshape(n_slots, width)
    peer_d_pre = swap(d_other, core)
    hub_got = swap(hub_send, core)
    peer_agg_t = swap(agg_t, core)

    xy_rows, z_rows = width // n_xy, width // n_xy // n_z
    hub_xy, hub_z = n_hubs // 2 // n_xy, n_hubs // 2 // n_xy // n_z

    def across(parts, bits, first=1):
        return [swap(part, spread(bits, first + k)) for k, part in enumerate(parts)]

    def in_order(values, earlier):
        return list(lax.optimization_barrier((*values, *earlier))[: len(values)])

    def start_sum(own, peer, hub_in):
        extra = 2 * hub_xy if hub_in else 0
        return run_inside(
            functools.partial(weight_body, n_xy, bool(hub_in)),
            xy_me[None],
            [own, peer, d_pre, peer_d_pre] + hub_in,
            [((xy_rows, half), F32)]
            + [((xy_rows + extra, half), BF16)] * (n_xy - 1)
            + ([((2, hub_xy, half), F32)] if hub_in else []),
            flops=4 * width * half * n_local,
            scratch=[pltpu.VMEM((width, half), F32)],
        )

    def fold(keep, hub_in, got):
        extra = 2 * hub_z if hub_in else 0
        return run_inside(
            functools.partial(fold_body, n_z, bool(hub_in)),
            z_me[None],
            [keep] + hub_in + got,
            [((z_rows, half), F32)]
            + [((z_rows + extra, half), BF16)] * (n_z - 1)
            + ([((2, hub_z, half), F32)] if hub_in else []),
            scratch=[pltpu.VMEM((xy_rows, half), F32)],
        )

    self_xy = start_sum(feat_t, peer_feat_t, [])
    self_got = across(self_xy[1:], xy_bits)
    agg_pair = in_order([agg_t, peer_agg_t], self_xy)
    neigh_xy = start_sum(*agg_pair, [hub_keep, hub_got])
    neigh_got = across(neigh_xy[1:n_xy], xy_bits)
    self_z = fold(self_xy[0], [], self_got)
    self_got = across(self_z[1:], z_bits)
    neigh_got = in_order(neigh_got, self_got)
    neigh_z = fold(neigh_xy[0], [neigh_xy[n_xy]], neigh_got)
    neigh_got = across(neigh_z[1:n_z], z_bits)
    own, hub_back = run_inside(
        functools.partial(last_body, n_z - 1),
        z_me[None],
        [self_z[0], neigh_z[0], neigh_z[n_z]] + self_got + neigh_got,
        [((2 * z_rows, half), BF16), ((2, hub_z, half), F32)],
    )

    line = [own] + across([own] * (n_z - 1), z_bits)
    n_share = 2
    n_piece = n_z // n_share
    got = []
    for share in range(n_share):
        (piece,) = run_inside(
            join_body,
            z_me[None],
            line[share * n_piece : (share + 1) * n_piece],
            [((n_piece * 2 * z_rows, half), BF16)],
        )
        if share > 0:
            (piece,) = in_order([piece], got[-1])
        got.append([piece] + across([piece] * (n_xy - 1), xy_bits))
    (grad_x,) = run(
        node_body,
        side[None],
        [w_self, d_pre, d_other, counts_own_t, d_agg, chosen, returned, hub_row, hub_back],
        [(wide, BF16)],
        flops=2 * n_local * width * (width + n_local + n_slots),
    )
    got[-1] = in_order(got[-1], [grad_x])
    blocks = [one for share in got for one in share]
    grad_self, grad_neigh = run_inside(
        functools.partial(place_body, n_xy, n_z, n_share),
        jnp.stack([side, xy_me, z_me]),
        blocks + [swap(one, core) for one in blocks],
        [((width, width), BF16)] * 2,
    )
    return hidden, grad_x, grad_self, grad_neigh


def solution(mesh):
    split = P(AXES, None)
    in_specs = (split, split, P(AXES), split, split, P(AXES), P(), P(), P(), split)
    out_specs = (split, split, P(), P())
    return jax.shard_map(
        on_device, mesh=mesh, in_specs=in_specs, out_specs=out_specs, check_vma=False
    )
```

```python
import functools

import jax
import jax.numpy as jnp
from jax import lax
from jax.experimental import pallas as pl
from jax.experimental.pallas import tpu as pltpu
from jax.sharding import PartitionSpec as P

AXES = ("row", "col")
BF16 = jnp.bfloat16
F32 = jnp.float32
CHUNK = 512
HBM = pl.BlockSpec(memory_space=pl.ANY)
VMEM_LIMIT = 56 << 20
VMEM = pl.BlockSpec(memory_space=pltpu.VMEM)
SMEM = pl.BlockSpec(memory_space=pltpu.SMEM)


def mul(left, right):
    return jnp.dot(left, right, preferred_element_type=F32)


def mul_t(left, right):
    return lax.dot_general(left, right, (((1,), (1,)), ((), ())), preferred_element_type=F32)


def t_mul(left, right):
    return lax.dot_general(left, right, (((0,), (0,)), ((), ())), preferred_element_type=F32)


def run(body, scalars, ins, outs, flops=0, scratch=(), limit=0):
    n_in, n_out = len(ins), len(outs)
    outs = [jax.ShapeDtypeStruct(shape, dtype) for shape, dtype in outs]

    def kernel(*refs):
        scalar_ref, refs = refs[0], refs[1:]
        in_hbm, out_hbm = refs[:n_in], refs[n_in : n_in + n_out]
        refs = refs[n_in + n_out :]
        in_buf, out_buf = refs[:n_in], refs[n_in : n_in + n_out]
        extra, (in_sem, out_sem) = refs[n_in + n_out : -2], refs[-2:]
        loads = [pltpu.make_async_copy(in_hbm[i], in_buf[i], in_sem.at[i]) for i in range(n_in)]
        stores = [pltpu.make_async_copy(out_buf[i], out_hbm[i], out_sem.at[i]) for i in range(n_out)]
        for load in loads:
            load.start()

        def need(*which):
            for i in which:
                loads[i].wait()

        def emit(*which):
            for i in which:
                stores[i].start()

        body(scalar_ref, in_buf, out_buf, need, emit, *extra)
        for store in stores:
            store.wait()

    held = sum(a.size * a.dtype.itemsize for a in [*ins, *outs])
    return pl.pallas_call(
        kernel,
        out_shape=outs,
        in_specs=[SMEM] + [HBM] * n_in,
        out_specs=[HBM] * n_out,
        scratch_shapes=[pltpu.VMEM(a.shape, a.dtype) for a in [*ins, *outs]]
        + list(scratch)
        + [pltpu.SemaphoreType.DMA((n_in,)), pltpu.SemaphoreType.DMA((n_out,))],
        compiler_params=pltpu.CompilerParams(vmem_limit_bytes=limit or held + (8 << 20)),
        cost_estimate=pl.CostEstimate(flops=0, bytes_accessed=0, transcendentals=0),
    )(scalars, *ins)


def run_inside(body, scalars, ins, outs, flops=0, scratch=()):
    n_in, n_out = len(ins), len(outs)
    outs = [jax.ShapeDtypeStruct(shape, dtype) for shape, dtype in outs]

    def kernel(*refs):
        body(refs[0], refs[1 : 1 + n_in], refs[1 + n_in : 1 + n_in + n_out], *refs[1 + n_in + n_out :])

    held = sum(a.size * a.dtype.itemsize for a in [*ins, *outs])
    return pl.pallas_call(
        kernel,
        out_shape=outs,
        in_specs=[SMEM] + [VMEM] * n_in,
        out_specs=[VMEM] * n_out,
        scratch_shapes=list(scratch),
        compiler_params=pltpu.CompilerParams(vmem_limit_bytes=held + (8 << 20)),
        cost_estimate=pl.CostEstimate(flops=0, bytes_accessed=0, transcendentals=0),
    )(scalars, *ins)


def one_hot(ids, n_local):
    rows = lax.broadcasted_iota(jnp.int32, (n_local, ids.shape[1]), 0)
    return (rows == ids).astype(F32).astype(BF16)


def pack_body(scalars, ins, outs, need, emit):
    features, send_rows, send_count, hub_rows = ins
    outgoing, own_hubs, chosen = outs
    n_local = features.shape[0]
    n_slots, n_dev = send_rows.shape[1], send_count.shape[1]
    capacity = n_slots // n_dev
    need(1, 2, 3)
    peer = lax.broadcasted_iota(jnp.int32, (n_dev, n_slots), 0)
    lane = lax.broadcasted_iota(jnp.int32, (n_dev, n_slots), 1)
    spread = (lane // capacity == peer).astype(F32)
    live = mul(send_count[...].astype(F32), spread)
    slot = lax.broadcasted_iota(jnp.int32, (1, n_slots), 1) % capacity
    ids = jnp.where(slot.astype(F32) < live, send_rows[...], -1)
    chosen[...] = ids
    emit(2)
    pick = one_hot(ids, n_local)
    pick_hub = one_hot(hub_rows[...], n_local)
    need(0)
    own_hubs[...] = t_mul(pick_hub, features[...]).astype(BF16)
    emit(1)
    outgoing[...] = t_mul(pick, features[...]).astype(BF16)
    emit(0)


def seed_body(side, ins, outs, need, emit, d_pre_all, aggregate):
    counts, arrived, hubs, summed, inv_deg, w_neigh, own_pre, cotangent, counts_t = ins
    hidden, d_pre, d_agg, d_pre_other, aggregate_t, d_arrived, hub_keep, hub_send = outs
    n_local, width = cotangent.shape
    n_slots = arrived.shape[0]
    n_hubs = hubs.shape[0]
    half = width // 2
    need(0, 1, 2, 3, 4)
    inv = inv_deg[...]
    for c in range(0, width, CHUNK):
        cols = slice(c, c + CHUNK)
        total = summed[:, cols] + mul(counts[:, :n_slots], arrived[:, cols])
        total = total + mul(counts[:, n_slots:], hubs[:, cols])
        mean = total * inv
        aggregate[:, cols] = mean.astype(BF16)
        aggregate_t[cols, :] = mean.T.astype(BF16)
    emit(4)
    need(5, 6, 7)
    for c in range(0, width, CHUNK):
        cols = slice(c, c + CHUNK)
        pre = own_pre[:, cols] + mul(aggregate[...], w_neigh[:, cols])
        sig = 0.5 + 0.5 * jnp.tanh(0.5 * pre)
        hidden[:, cols] = (pre * sig).astype(BF16)
        grad = cotangent[:, cols].astype(F32) * (sig * (1.0 + pre * (1.0 - sig)))
        grad = grad.astype(BF16)
        d_pre_all[:, cols] = grad
        part = slice(c % half, c % half + CHUNK)

        @pl.when(side[0] == c // half)
        def _():
            d_pre[:, part] = grad

        @pl.when(side[0] != c // half)
        def _():
            d_pre_other[:, part] = grad

    emit(3, 1, 0)
    need(8)
    for c in range(0, width, CHUNK):
        cols = slice(c, c + CHUNK)
        grad = (mul_t(d_pre_all[...], w_neigh[cols, :]) * inv).astype(BF16)
        d_agg[:, cols] = grad
        d_arrived[:, cols] = mul(counts_t[:n_slots, :], grad).astype(BF16)
        d_hubs = mul(counts_t[n_slots:, :], grad)
        part = slice(c % half, c % half + CHUNK)
        hub_keep[c // half, :, part] = d_hubs[: n_hubs // 2]
        hub_send[c // half, :, part] = d_hubs[n_hubs // 2 :].astype(BF16)
    emit(5, 7, 6, 2)


def hub_rows_of(total, k, rows):
    return jnp.concatenate([total[0, k * rows : (k + 1) * rows], total[1, k * rows : (k + 1) * rows]], 0)


def weight_body(n_part, with_hubs, mine, ins, outs, total):
    own, peer, d_own, d_peer = ins[:4]
    rows, half = outs[0].shape
    total[...] = mul(own[...], d_own[...]) + mul(peer[...], d_peer[...])
    if with_hubs:
        hubs = ins[4][...] + ins[5][...].astype(F32)
        size = hubs.shape[1] // n_part
        outs[n_part][...] = hubs[:, :size]
    for k in range(n_part):
        at = pl.ds(pl.multiple_of((mine[0] ^ k) * rows, rows), rows)
        outs[k][:rows, :] = total[at, :].astype(outs[k].dtype)
        if k > 0 and with_hubs:
            outs[k][rows:, :] = hub_rows_of(hubs, k, size).astype(BF16)


def add_up(keep, hubs, got):
    size = keep.shape[0]
    value = keep[...]
    for one in got:
        value = value + one[:size, :].astype(F32)
    if hubs is None:
        return value, None, None
    first, second = hubs[0], hubs[1]
    n_hub = first.shape[0]
    for one in got:
        tail = one[size:, :].astype(F32)
        first = first + tail[:n_hub]
        second = second + tail[n_hub:]
    return value, first, second


def fold_body(n_part, with_hubs, mine, ins, outs, total):
    hubs = ins[1] if with_hubs else None
    rows = outs[0].shape[0]
    value, first, second = add_up(ins[0], hubs, ins[1 + int(with_hubs) :])
    total[...] = value
    if with_hubs:
        n_hub = first.shape[0] // n_part
        outs[n_part][0] = first[:n_hub]
        outs[n_part][1] = second[:n_hub]
    for k in range(n_part):
        at = pl.ds(pl.multiple_of((mine[0] ^ k) * rows, rows), rows)
        outs[k][:rows, :] = total[at, :].astype(outs[k].dtype)
        if k > 0 and with_hubs:
            span = slice(k * n_hub, (k + 1) * n_hub)
            outs[k][rows:, :] = jnp.concatenate([first[span], second[span]], 0).astype(BF16)


def last_body(with_hubs, scalars, ins, outs):
    hubs = ins[1] if with_hubs else None
    value, first, second = add_up(ins[0], hubs, ins[1 + int(with_hubs) :])
    outs[0][...] = value.astype(BF16)
    if with_hubs:
        outs[1][0] = first
        outs[1][1] = second


def join_body(scalars, ins, outs):
    at = 0
    for one in ins:
        outs[0][at : at + one.shape[0], :] = one[...]
        at += one.shape[0]


def node_body(side, ins, outs, need, emit):
    w_self, d_pre, d_other, counts_t, d_agg, chosen, returned, hub_rows, hub_back = ins
    (grad_x,) = outs
    n_local = d_pre.shape[0]
    width = w_self.shape[0]
    half = width // 2
    need(*range(len(ins)))
    picked = one_hot(chosen[...], n_local)
    hub_picked = one_hot(hub_rows[...], n_local)
    mine = pl.ds(pl.multiple_of(side[0] * half, half), half)
    theirs = pl.ds(pl.multiple_of((1 - side[0]) * half, half), half)
    for c in range(0, width, CHUNK):
        cols = slice(c, c + CHUNK)
        part = slice(c % half, c % half + CHUNK)
        back = hub_back[c // half, :, part]
        high = back.astype(BF16)
        low = (back - high.astype(F32)).astype(BF16)
        total = mul_t(d_pre[...], w_self[cols, mine]) + mul_t(d_other[...], w_self[cols, theirs])
        total = total + mul(counts_t[...], d_agg[:, cols])
        total = total + mul(picked, returned[:, cols])
        total = total + mul(hub_picked, high) + mul(hub_picked, low)
        grad_x[:, cols] = total.astype(BF16)
    emit(0)


def place_body(n_xy, n_z, where, ins, outs):
    half = ins[0].shape[1]
    rows = ins[0].shape[0] // n_z
    for i, block in enumerate(ins):
        core, k = divmod(i, n_xy)
        cols = pl.ds(pl.multiple_of((where[0] ^ core) * half, half), half)
        for j in range(n_z):
            at = pl.ds(pl.multiple_of(((where[1] ^ k) * n_z + (where[2] ^ j)) * rows, rows), rows)
            outs[0][at, cols] = block[j * rows : (j + 1) * rows, :]


def on_device(
    features,
    neighbours,
    degrees,
    send_rows,
    send_count,
    hub_rows,
    w_self,
    w_neigh,
    bias_term,
    cotangent,
):
    n_row = lax.axis_size("row")
    n_col = lax.axis_size("col")
    n_dev = n_row * n_col
    me = lax.axis_index("row") * n_col + lax.axis_index("col")
    n_local, width = features.shape
    fanout = neighbours.shape[1]
    n_slots = send_rows.shape[1]
    capacity = n_slots // n_dev
    n_hub = hub_rows.shape[0]
    n_hubs = n_dev * n_hub
    half = width // 2
    hub_base = n_local + n_slots
    wide = (n_local, width)

    core = n_col
    xy_bits = [1] + [n_col << i for i in range(1, n_row.bit_length() - 1)]
    z_bits = [1 << i for i in range(1, n_col.bit_length() - 1)]
    hub_bits = z_bits + xy_bits + [core]
    n_xy, n_z = 1 << len(xy_bits), 1 << len(z_bits)

    def spread(bits, k):
        return sum(mask for i, mask in enumerate(bits) if k >> i & 1)

    def bit(mask):
        return (me & mask) // mask

    def place_of(bits):
        return sum(bit(mask) << i for i, mask in enumerate(bits))

    def swap(value, mask):
        return lax.ppermute(value, AXES, [(i, i ^ mask) for i in range(n_dev)])

    side, xy_me, z_me = bit(core), place_of(xy_bits), place_of(z_bits)

    hub_row = hub_rows.reshape(1, n_hub)
    outgoing, own_hubs, chosen = run(
        pack_body,
        side[None],
        [features, send_rows, send_count, hub_row],
        [((n_slots, width), BF16), ((n_hub, width), BF16), ((1, n_slots), jnp.int32)],
        flops=2 * n_slots * n_local * width,
        limit=VMEM_LIMIT,
    )
    arrived = lax.all_to_all(
        outgoing.reshape(n_dev, capacity, width), AXES, split_axis=0, concat_axis=0, tiled=True
    ).reshape(n_slots, width)

    hubs = jnp.concatenate([own_hubs] + [swap(own_hubs, spread(z_bits, k)) for k in range(1, n_z)], 0)
    for mask in xy_bits + [core]:
        hubs = jnp.concatenate([hubs, swap(hubs, mask)], 0)
    feat_t = features.T
    peer_feat_t = swap(feat_t, core)

    hub_id = neighbours - hub_base
    relative = (hub_id // n_hub) ^ me
    spot = sum(((relative & mask) // mask) << i for i, mask in enumerate(hub_bits))
    where_to = jnp.where(hub_id >= 0, hub_base + spot * n_hub + hub_id % n_hub, neighbours)
    where_to = jnp.where(jnp.arange(fanout, dtype=jnp.int32)[None, :] < degrees[:, None], where_to, -1)
    to_t = where_to.T

    def count(first, last):
        ids = jnp.arange(first, last, dtype=jnp.int32)
        found = sum((where_to[:, j : j + 1] == ids[None, :]).astype(F32) for j in range(fanout))
        found_t = sum((to_t[j : j + 1, :] == ids[:, None]).astype(F32) for j in range(fanout))
        return found.astype(BF16), found_t.astype(BF16)

    counts_own, counts_own_t = count(0, n_local)
    counts_far, counts_far_t = count(n_local, hub_base + n_hubs)
    inv_deg = 1.0 / degrees.astype(F32)[:, None]
    summed = mul(counts_own, features)
    own_pre = mul(features, w_self) + bias_term[None, :]

    hidden, d_pre, d_agg, d_other, agg_t, d_arrived, hub_keep, hub_send = run(
        seed_body,
        side[None],
        [counts_far, arrived, hubs, summed, inv_deg, w_neigh, own_pre, cotangent, counts_far_t],
        [
            (wide, BF16),
            ((n_local, half), BF16),
            (wide, BF16),
            ((n_local, half), BF16),
            ((width, n_local), BF16),
            ((n_slots, width), BF16),
            ((2, n_hubs // 2, half), F32),
            ((2, n_hubs // 2, half), BF16),
        ],
        flops=4 * n_local * width * (width + n_slots + n_hubs),
        scratch=[pltpu.VMEM(wide, BF16), pltpu.VMEM(wide, BF16)],
        limit=VMEM_LIMIT,
    )
    returned = lax.all_to_all(
        d_arrived.reshape(n_dev, capacity, width), AXES, split_axis=0, concat_axis=0, tiled=True
    ).reshape(n_slots, width)
    peer_d_pre = swap(d_other, core)
    hub_got = swap(hub_send, core)
    peer_agg_t = swap(agg_t, core)

    xy_rows, z_rows = width // n_xy, width // n_xy // n_z
    hub_xy, hub_z = n_hubs // 2 // n_xy, n_hubs // 2 // n_xy // n_z

    def across(parts, bits, first=1):
        return [swap(part, spread(bits, first + k)) for k, part in enumerate(parts)]

    def in_order(values, earlier):
        return list(lax.optimization_barrier((*values, *earlier))[: len(values)])

    def start_sum(own, peer, hub_in):
        extra = 2 * hub_xy if hub_in else 0
        return run_inside(
            functools.partial(weight_body, n_xy, bool(hub_in)),
            xy_me[None],
            [own, peer, d_pre, peer_d_pre] + hub_in,
            [((xy_rows, half), F32)]
            + [((xy_rows + extra, half), BF16)] * (n_xy - 1)
            + ([((2, hub_xy, half), F32)] if hub_in else []),
            flops=4 * width * half * n_local,
            scratch=[pltpu.VMEM((width, half), F32)],
        )

    def fold(keep, hub_in, got):
        extra = 2 * hub_z if hub_in else 0
        return run_inside(
            functools.partial(fold_body, n_z, bool(hub_in)),
            z_me[None],
            [keep] + hub_in + got,
            [((z_rows, half), F32)]
            + [((z_rows + extra, half), BF16)] * (n_z - 1)
            + ([((2, hub_z, half), F32)] if hub_in else []),
            scratch=[pltpu.VMEM((xy_rows, half), F32)],
        )

    self_xy = start_sum(feat_t, peer_feat_t, [])
    self_got = across(self_xy[1:], xy_bits)
    agg_pair = in_order([agg_t, peer_agg_t], self_xy)
    neigh_xy = start_sum(*agg_pair, [hub_keep, hub_got])
    neigh_got = across(neigh_xy[1:n_xy], xy_bits)
    self_got = in_order(self_got, neigh_xy)
    self_z = fold(self_xy[0], [], self_got)
    self_got = across(self_z[1:], z_bits)
    neigh_got = in_order(neigh_got, self_got)
    neigh_z = fold(neigh_xy[0], [neigh_xy[n_xy]], neigh_got)
    neigh_got = across(neigh_z[1:n_z], z_bits)

    def finish(keep, hub_in, got):
        return run_inside(
            functools.partial(last_body, bool(hub_in)),
            z_me[None],
            [keep] + hub_in + got,
            [((z_rows, half), BF16)] + ([((2, hub_z, half), F32)] if hub_in else []),
        )

    def gather_line(own):
        pieces = [own] + across([own] * (n_z - 1), z_bits)
        return run_inside(join_body, z_me[None], pieces, [((xy_rows, half), BF16)])[0]

    def place(blocks):
        return run_inside(
            functools.partial(place_body, n_xy, n_z),
            jnp.stack([side, xy_me, z_me]),
            blocks + [swap(one, core) for one in blocks],
            [((width, width), BF16)],
        )[0]

    (self_own,) = finish(self_z[0], [], self_got)
    neigh_own, hub_back = finish(neigh_z[0], [neigh_z[n_z]], neigh_got)
    self_line = gather_line(self_own)
    self_blocks = [self_line] + across([self_line] * (n_xy - 1), xy_bits)
    neigh_line = gather_line(neigh_own)
    (neigh_line,) = in_order([neigh_line], self_blocks)
    neigh_blocks = [neigh_line] + across([neigh_line] * (n_xy - 1), xy_bits)
    grad_self = place(self_blocks)
    (grad_x,) = run(
        node_body,
        side[None],
        [w_self, d_pre, d_other, counts_own_t, d_agg, chosen, returned, hub_row, hub_back],
        [(wide, BF16)],
        flops=2 * n_local * width * (width + n_local + n_slots),
    )
    grad_neigh = place(in_order(neigh_blocks, [grad_x, grad_self]))
    return hidden, grad_x, grad_self, grad_neigh


def solution(mesh):
    split = P(AXES, None)
    in_specs = (split, split, P(AXES), split, split, P(AXES), P(), P(), P(), split)
    out_specs = (split, split, P(), P())
    return jax.shard_map(
        on_device, mesh=mesh, in_specs=in_specs, out_specs=out_specs, check_vma=False
    )
```

```python
import functools

import jax
import jax.numpy as jnp
from jax import lax
from jax.experimental import pallas as pl
from jax.experimental.pallas import tpu as pltpu
from jax.sharding import PartitionSpec as P

AXES = ("row", "col")
BF16 = jnp.bfloat16
F32 = jnp.float32
CHUNK = 512
HBM = pl.BlockSpec(memory_space=pl.ANY)
VMEM_LIMIT = 56 << 20
VMEM = pl.BlockSpec(memory_space=pltpu.VMEM)
SMEM = pl.BlockSpec(memory_space=pltpu.SMEM)


def mul(left, right):
    return jnp.dot(left, right, preferred_element_type=F32)


def mul_t(left, right):
    return lax.dot_general(left, right, (((1,), (1,)), ((), ())), preferred_element_type=F32)


def t_mul(left, right):
    return lax.dot_general(left, right, (((0,), (0,)), ((), ())), preferred_element_type=F32)


def run(body, scalars, ins, outs, flops=0, scratch=(), limit=0):
    n_in, n_out = len(ins), len(outs)
    outs = [jax.ShapeDtypeStruct(shape, dtype) for shape, dtype in outs]

    def kernel(*refs):
        scalar_ref, refs = refs[0], refs[1:]
        in_hbm, out_hbm = refs[:n_in], refs[n_in : n_in + n_out]
        refs = refs[n_in + n_out :]
        in_buf, out_buf = refs[:n_in], refs[n_in : n_in + n_out]
        extra, (in_sem, out_sem) = refs[n_in + n_out : -2], refs[-2:]
        loads = [pltpu.make_async_copy(in_hbm[i], in_buf[i], in_sem.at[i]) for i in range(n_in)]
        stores = [pltpu.make_async_copy(out_buf[i], out_hbm[i], out_sem.at[i]) for i in range(n_out)]
        for load in loads:
            load.start()

        def need(*which):
            for i in which:
                loads[i].wait()

        def emit(*which):
            for i in which:
                stores[i].start()

        body(scalar_ref, in_buf, out_buf, need, emit, *extra)
        for store in stores:
            store.wait()

    held = sum(a.size * a.dtype.itemsize for a in [*ins, *outs])
    return pl.pallas_call(
        kernel,
        out_shape=outs,
        in_specs=[SMEM] + [HBM] * n_in,
        out_specs=[HBM] * n_out,
        scratch_shapes=[pltpu.VMEM(a.shape, a.dtype) for a in [*ins, *outs]]
        + list(scratch)
        + [pltpu.SemaphoreType.DMA((n_in,)), pltpu.SemaphoreType.DMA((n_out,))],
        compiler_params=pltpu.CompilerParams(vmem_limit_bytes=limit or held + (8 << 20)),
        cost_estimate=pl.CostEstimate(flops=0, bytes_accessed=0, transcendentals=0),
    )(scalars, *ins)


def run_inside(body, scalars, ins, outs, flops=0, scratch=()):
    n_in, n_out = len(ins), len(outs)
    outs = [jax.ShapeDtypeStruct(shape, dtype) for shape, dtype in outs]

    def kernel(*refs):
        body(refs[0], refs[1 : 1 + n_in], refs[1 + n_in : 1 + n_in + n_out], *refs[1 + n_in + n_out :])

    held = sum(a.size * a.dtype.itemsize for a in [*ins, *outs])
    return pl.pallas_call(
        kernel,
        out_shape=outs,
        in_specs=[SMEM] + [VMEM] * n_in,
        out_specs=[VMEM] * n_out,
        scratch_shapes=list(scratch),
        compiler_params=pltpu.CompilerParams(vmem_limit_bytes=held + (8 << 20)),
        cost_estimate=pl.CostEstimate(flops=0, bytes_accessed=0, transcendentals=0),
    )(scalars, *ins)


def one_hot(ids, n_local):
    rows = lax.broadcasted_iota(jnp.int32, (n_local, ids.shape[1]), 0)
    return (rows == ids).astype(F32).astype(BF16)


def pack_body(scalars, ins, outs, need, emit):
    features, send_rows, send_count, hub_rows = ins
    outgoing, own_hubs, chosen = outs
    n_local = features.shape[0]
    n_slots, n_dev = send_rows.shape[1], send_count.shape[1]
    capacity = n_slots // n_dev
    need(1, 2, 3)
    peer = lax.broadcasted_iota(jnp.int32, (n_dev, n_slots), 0)
    lane = lax.broadcasted_iota(jnp.int32, (n_dev, n_slots), 1)
    spread = (lane // capacity == peer).astype(F32)
    live = mul(send_count[...].astype(F32), spread)
    slot = lax.broadcasted_iota(jnp.int32, (1, n_slots), 1) % capacity
    ids = jnp.where(slot.astype(F32) < live, send_rows[...], -1)
    chosen[...] = ids
    emit(2)
    pick = one_hot(ids, n_local)
    pick_hub = one_hot(hub_rows[...], n_local)
    need(0)
    own_hubs[...] = t_mul(pick_hub, features[...]).astype(BF16)
    emit(1)
    outgoing[...] = t_mul(pick, features[...]).astype(BF16)
    emit(0)


def seed_body(side, ins, outs, need, emit, d_pre_all, aggregate):
    counts, arrived, hubs, summed, inv_deg, w_neigh, own_pre, cotangent, counts_t = ins
    hidden, d_pre, d_agg, d_pre_other, aggregate_t, d_arrived, hub_keep, hub_send = outs
    n_local, width = cotangent.shape
    n_slots = arrived.shape[0]
    n_hubs = hubs.shape[0]
    half = width // 2
    need(0, 1, 2, 3, 4)
    inv = inv_deg[...]
    for c in range(0, width, CHUNK):
        cols = slice(c, c + CHUNK)
        total = summed[:, cols] + mul(counts[:, :n_slots], arrived[:, cols])
        total = total + mul(counts[:, n_slots:], hubs[:, cols])
        mean = total * inv
        aggregate[:, cols] = mean.astype(BF16)
        aggregate_t[cols, :] = mean.T.astype(BF16)
    emit(4)
    need(5, 6, 7)
    for c in range(0, width, CHUNK):
        cols = slice(c, c + CHUNK)
        pre = own_pre[:, cols] + mul(aggregate[...], w_neigh[:, cols])
        sig = 0.5 + 0.5 * jnp.tanh(0.5 * pre)
        hidden[:, cols] = (pre * sig).astype(BF16)
        grad = cotangent[:, cols].astype(F32) * (sig * (1.0 + pre * (1.0 - sig)))
        grad = grad.astype(BF16)
        d_pre_all[:, cols] = grad
        part = slice(c % half, c % half + CHUNK)

        @pl.when(side[0] == c // half)
        def _():
            d_pre[:, part] = grad

        @pl.when(side[0] != c // half)
        def _():
            d_pre_other[:, part] = grad

    emit(3, 1, 0)
    need(8)
    for c in range(0, width, CHUNK):
        cols = slice(c, c + CHUNK)
        grad = (mul_t(d_pre_all[...], w_neigh[cols, :]) * inv).astype(BF16)
        d_agg[:, cols] = grad
        d_arrived[:, cols] = mul(counts_t[:n_slots, :], grad).astype(BF16)
        d_hubs = mul(counts_t[n_slots:, :], grad)
        part = slice(c % half, c % half + CHUNK)
        hub_keep[c // half, :, part] = d_hubs[: n_hubs // 2]
        hub_send[c // half, :, part] = d_hubs[n_hubs // 2 :].astype(BF16)
    emit(5, 7, 6, 2)


def hub_rows_of(total, k, rows):
    return jnp.concatenate([total[0, k * rows : (k + 1) * rows], total[1, k * rows : (k + 1) * rows]], 0)


def weight_body(n_part, with_hubs, mine, ins, outs, total):
    own, peer, d_own, d_peer = ins[:4]
    rows, half = outs[0].shape
    total[...] = mul(own[...], d_own[...]) + mul(peer[...], d_peer[...])
    if with_hubs:
        hubs = ins[4][...] + ins[5][...].astype(F32)
        size = hubs.shape[1] // n_part
        outs[n_part][...] = hubs[:, :size]
    for k in range(n_part):
        at = pl.ds(pl.multiple_of((mine[0] ^ k) * rows, rows), rows)
        outs[k][:rows, :] = total[at, :].astype(outs[k].dtype)
        if k > 0 and with_hubs:
            outs[k][rows:, :] = hub_rows_of(hubs, k, size).astype(BF16)


def add_up(keep, hubs, got):
    size = keep.shape[0]
    value = keep[...]
    for one in got:
        value = value + one[:size, :].astype(F32)
    if hubs is None:
        return value, None, None
    first, second = hubs[0], hubs[1]
    n_hub = first.shape[0]
    for one in got:
        tail = one[size:, :].astype(F32)
        first = first + tail[:n_hub]
        second = second + tail[n_hub:]
    return value, first, second


def halve_body(with_hubs, at_bit, where, ins, outs, total):
    hubs = ins[1] if with_hubs else None
    value, first, second = add_up(ins[0], hubs, ins[1 + int(with_hubs) :])
    total[...] = value
    keep, send = outs[:2]
    rows = keep.shape[0]
    mine = where[at_bit]
    keep[...] = total[pl.ds(pl.multiple_of(mine * rows, rows), rows), :]
    send[:rows, :] = total[pl.ds(pl.multiple_of((1 - mine) * rows, rows), rows), :].astype(BF16)
    if with_hubs:
        n_hub = first.shape[0] // 2
        outs[2][0] = first[:n_hub]
        outs[2][1] = second[:n_hub]
        send[rows:, :] = jnp.concatenate([first[n_hub:], second[n_hub:]], 0).astype(BF16)


def meet_body(with_hubs, where, ins, outs):
    hubs = ins[1] if with_hubs else None
    value, first, second = add_up(ins[0], hubs, ins[1 + int(with_hubs) :])
    rows = value.shape[0]
    outs[0][:rows, :] = value.astype(BF16)
    if with_hubs:
        n_hub = first.shape[0] // 2
        outs[1][0] = first[:n_hub]
        outs[1][1] = second[:n_hub]
        outs[0][rows:, :] = jnp.concatenate([first[n_hub:], second[n_hub:]], 0).astype(BF16)


def close_body(with_hubs, where, ins, outs):
    rows = outs[0].shape[0]
    own, got = ins[0], ins[1]
    outs[0][...] = (own[:rows, :].astype(F32) + got[:rows, :].astype(F32)).astype(BF16)
    if with_hubs:
        tail = got[rows:, :].astype(F32)
        n_hub = tail.shape[0] // 2
        outs[1][0] = ins[2][0] + tail[:n_hub]
        outs[1][1] = ins[2][1] + tail[n_hub:]


def join_body(scalars, ins, outs):
    at = 0
    for one in ins:
        outs[0][at : at + one.shape[0], :] = one[...]
        at += one.shape[0]


def node_body(side, ins, outs, need, emit):
    w_self, d_pre, d_other, counts_t, d_agg, chosen, returned, hub_rows, hub_back = ins
    (grad_x,) = outs
    n_local = d_pre.shape[0]
    width = w_self.shape[0]
    half = width // 2
    need(*range(len(ins)))
    picked = one_hot(chosen[...], n_local)
    hub_picked = one_hot(hub_rows[...], n_local)
    mine = pl.ds(pl.multiple_of(side[0] * half, half), half)
    theirs = pl.ds(pl.multiple_of((1 - side[0]) * half, half), half)
    for c in range(0, width, CHUNK):
        cols = slice(c, c + CHUNK)
        part = slice(c % half, c % half + CHUNK)
        back = hub_back[c // half, :, part]
        high = back.astype(BF16)
        low = (back - high.astype(F32)).astype(BF16)
        total = mul_t(d_pre[...], w_self[cols, mine]) + mul_t(d_other[...], w_self[cols, theirs])
        total = total + mul(counts_t[...], d_agg[:, cols])
        total = total + mul(picked, returned[:, cols])
        total = total + mul(hub_picked, high) + mul(hub_picked, low)
        grad_x[:, cols] = total.astype(BF16)
    emit(0)


def place_body(n_xy, n_z, where, ins, outs):
    half = ins[0].shape[1]
    rows = ins[0].shape[0] // n_z
    for i, block in enumerate(ins):
        core, k = divmod(i, n_xy)
        cols = pl.ds(pl.multiple_of((where[0] ^ core) * half, half), half)
        for j in range(n_z):
            at = pl.ds(pl.multiple_of(((where[1] ^ k) * n_z + (where[2] ^ j)) * rows, rows), rows)
            outs[0][at, cols] = block[j * rows : (j + 1) * rows, :]


def on_device(
    features,
    neighbours,
    degrees,
    send_rows,
    send_count,
    hub_rows,
    w_self,
    w_neigh,
    bias_term,
    cotangent,
):
    n_row = lax.axis_size("row")
    n_col = lax.axis_size("col")
    n_dev = n_row * n_col
    me = lax.axis_index("row") * n_col + lax.axis_index("col")
    n_local, width = features.shape
    fanout = neighbours.shape[1]
    n_slots = send_rows.shape[1]
    capacity = n_slots // n_dev
    n_hub = hub_rows.shape[0]
    n_hubs = n_dev * n_hub
    half = width // 2
    hub_base = n_local + n_slots
    wide = (n_local, width)

    core = n_col
    xy_bits = [1] + [n_col << i for i in range(1, n_row.bit_length() - 1)]
    z_bits = [1 << i for i in range(1, n_col.bit_length() - 1)]
    hub_bits = z_bits[::-1] + xy_bits + [core]
    n_xy, n_z = 1 << len(xy_bits), 1 << len(z_bits)

    def spread(bits, k):
        return sum(mask for i, mask in enumerate(bits) if k >> i & 1)

    def bit(mask):
        return (me & mask) // mask

    def place_of(bits):
        return sum(bit(mask) << i for i, mask in enumerate(bits))

    def swap(value, mask):
        return lax.ppermute(value, AXES, [(i, i ^ mask) for i in range(n_dev)])

    side, xy_me, z_me = bit(core), place_of(xy_bits), place_of(z_bits[-2::-1])
    z_at = jnp.stack([bit(mask) for mask in z_bits])

    hub_row = hub_rows.reshape(1, n_hub)
    outgoing, own_hubs, chosen = run(
        pack_body,
        side[None],
        [features, send_rows, send_count, hub_row],
        [((n_slots, width), BF16), ((n_hub, width), BF16), ((1, n_slots), jnp.int32)],
        flops=2 * n_slots * n_local * width,
        limit=VMEM_LIMIT,
    )
    arrived = lax.all_to_all(
        outgoing.reshape(n_dev, capacity, width), AXES, split_axis=0, concat_axis=0, tiled=True
    ).reshape(n_slots, width)

    hubs = jnp.concatenate([own_hubs] + [swap(own_hubs, spread(z_bits[::-1], k)) for k in range(1, n_z)], 0)
    for mask in xy_bits + [core]:
        hubs = jnp.concatenate([hubs, swap(hubs, mask)], 0)
    feat_t = features.T
    peer_feat_t = swap(feat_t, core)

    hub_id = neighbours - hub_base
    relative = (hub_id // n_hub) ^ me
    spot = sum(((relative & mask) // mask) << i for i, mask in enumerate(hub_bits))
    where_to = jnp.where(hub_id >= 0, hub_base + spot * n_hub + hub_id % n_hub, neighbours)
    where_to = jnp.where(jnp.arange(fanout, dtype=jnp.int32)[None, :] < degrees[:, None], where_to, -1)
    to_t = where_to.T

    def count(first, last):
        ids = jnp.arange(first, last, dtype=jnp.int32)
        found = sum((where_to[:, j : j + 1] == ids[None, :]).astype(F32) for j in range(fanout))
        found_t = sum((to_t[j : j + 1, :] == ids[:, None]).astype(F32) for j in range(fanout))
        return found.astype(BF16), found_t.astype(BF16)

    counts_own, counts_own_t = count(0, n_local)
    counts_far, counts_far_t = count(n_local, hub_base + n_hubs)
    inv_deg = 1.0 / degrees.astype(F32)[:, None]
    summed = mul(counts_own, features)
    own_pre = mul(features, w_self) + bias_term[None, :]

    hidden, d_pre, d_agg, d_other, agg_t, d_arrived, hub_keep, hub_send = run(
        seed_body,
        side[None],
        [counts_far, arrived, hubs, summed, inv_deg, w_neigh, own_pre, cotangent, counts_far_t],
        [
            (wide, BF16),
            ((n_local, half), BF16),
            (wide, BF16),
            ((n_local, half), BF16),
            ((width, n_local), BF16),
            ((n_slots, width), BF16),
            ((2, n_hubs // 2, half), F32),
            ((2, n_hubs // 2, half), BF16),
        ],
        flops=4 * n_local * width * (width + n_slots + n_hubs),
        scratch=[pltpu.VMEM(wide, BF16), pltpu.VMEM(wide, BF16)],
        limit=VMEM_LIMIT,
    )
    returned = lax.all_to_all(
        d_arrived.reshape(n_dev, capacity, width), AXES, split_axis=0, concat_axis=0, tiled=True
    ).reshape(n_slots, width)
    peer_d_pre = swap(d_other, core)
    hub_got = swap(hub_send, core)
    peer_agg_t = swap(agg_t, core)

    xy_rows = width // n_xy
    hub_xy = n_hubs // 2 // n_xy

    def across(parts, bits, first=1):
        return [swap(part, spread(bits, first + k)) for k, part in enumerate(parts)]

    def in_order(values, earlier):
        return list(lax.optimization_barrier((*values, *earlier))[: len(values)])

    def start_sum(own, peer, hub_in):
        extra = 2 * hub_xy if hub_in else 0
        return run_inside(
            functools.partial(weight_body, n_xy, bool(hub_in)),
            xy_me[None],
            [own, peer, d_pre, peer_d_pre] + hub_in,
            [((xy_rows, half), F32)]
            + [((xy_rows + extra, half), BF16)] * (n_xy - 1)
            + ([((2, hub_xy, half), F32)] if hub_in else []),
            flops=4 * width * half * n_local,
            scratch=[pltpu.VMEM((width, half), F32)],
        )

    def halve(keep, hub_in, got, at_bit):
        rows = keep.shape[0] // 2
        n_hub = hub_in[0].shape[1] // 2 if hub_in else 0
        keep, send, *hub_in = run_inside(
            functools.partial(halve_body, bool(hub_in), at_bit),
            z_at,
            [keep] + hub_in + got,
            [((rows, half), F32), ((rows + 2 * n_hub, half), BF16)] + [((2, n_hub, half), F32)] * bool(hub_in),
            scratch=[pltpu.VMEM((2 * rows, half), F32)],
        )
        return keep, hub_in, [swap(send, z_bits[at_bit])]

    def sum_line(keep, hub_in, got):
        for at_bit in range(len(z_bits) - 1):
            keep, hub_in, got = halve(keep, hub_in, got, at_bit)
        rows = keep.shape[0]
        n_hub = hub_in[0].shape[1] // 2 if hub_in else 0
        hub_out = [((2, n_hub, half), F32)] * bool(hub_in)
        own, *hub_in = run_inside(
            functools.partial(meet_body, bool(hub_in)),
            z_at,
            [keep] + hub_in + got,
            [((rows + 2 * n_hub, half), BF16)] + hub_out,
        )
        return run_inside(
            functools.partial(close_body, bool(hub_in)),
            z_at,
            [own, swap(own, z_bits[-1])] + hub_in,
            [((rows, half), BF16)] + hub_out,
        )

    def gather_line(own):
        for mask in z_bits[-2::-1]:
            pair = [own, swap(own, mask)]
            (own,) = run_inside(join_body, z_at, pair, [((2 * own.shape[0], half), BF16)])
        return own

    self_xy = start_sum(feat_t, peer_feat_t, [])
    self_got = across(self_xy[1:], xy_bits)
    agg_pair = in_order([agg_t, peer_agg_t], self_xy)
    neigh_xy = start_sum(*agg_pair, [hub_keep, hub_got])
    neigh_got = across(neigh_xy[1:n_xy], xy_bits)
    self_got = in_order(self_got, neigh_xy)
    (self_own,) = sum_line(self_xy[0], [], self_got)
    neigh_own, hub_back = sum_line(neigh_xy[0], [neigh_xy[n_xy]], neigh_got)

    def place(blocks):
        return run_inside(
            functools.partial(place_body, n_xy, n_z // 2),
            jnp.stack([side, xy_me, z_me]),
            blocks + [swap(one, core) for one in blocks],
            [((width, width), BF16)],
        )[0]

    self_line = gather_line(self_own)
    self_blocks = [self_line] + across([self_line] * (n_xy - 1), xy_bits)
    neigh_line = gather_line(neigh_own)
    (neigh_line,) = in_order([neigh_line], self_blocks)
    neigh_blocks = [neigh_line] + across([neigh_line] * (n_xy - 1), xy_bits)
    grad_self = place(in_order(self_blocks, neigh_blocks[:1]))
    (grad_x,) = run(
        node_body,
        side[None],
        [w_self, d_pre, d_other, counts_own_t, d_agg, chosen, returned, hub_row, hub_back],
        [(wide, BF16)],
        flops=2 * n_local * width * (width + n_local + n_slots),
    )
    grad_neigh = place(in_order(neigh_blocks, [grad_x, grad_self]))
    return hidden, grad_x, grad_self, grad_neigh


def solution(mesh):
    split = P(AXES, None)
    in_specs = (split, split, P(AXES), split, split, P(AXES), P(), P(), P(), split)
    out_specs = (split, split, P(), P())
    return jax.shard_map(
        on_device, mesh=mesh, in_specs=in_specs, out_specs=out_specs, check_vma=False
    )
```

```python
import functools

import jax
import jax.numpy as jnp
from jax import lax
from jax.experimental import pallas as pl
from jax.experimental.pallas import tpu as pltpu
from jax.sharding import PartitionSpec as P

AXES = ("row", "col")
BF16 = jnp.bfloat16
F32 = jnp.float32
CHUNK = 512
HBM = pl.BlockSpec(memory_space=pl.ANY)
VMEM_LIMIT = 56 << 20
VMEM = pl.BlockSpec(memory_space=pltpu.VMEM)
SMEM = pl.BlockSpec(memory_space=pltpu.SMEM)


def mul(left, right):
    return jnp.dot(left, right, preferred_element_type=F32)


def mul_t(left, right):
    return lax.dot_general(left, right, (((1,), (1,)), ((), ())), preferred_element_type=F32)


def t_mul(left, right):
    return lax.dot_general(left, right, (((0,), (0,)), ((), ())), preferred_element_type=F32)


def run(body, scalars, ins, outs, flops=0, scratch=(), limit=0):
    n_in, n_out = len(ins), len(outs)
    outs = [jax.ShapeDtypeStruct(shape, dtype) for shape, dtype in outs]

    def kernel(*refs):
        scalar_ref, refs = refs[0], refs[1:]
        in_hbm, out_hbm = refs[:n_in], refs[n_in : n_in + n_out]
        refs = refs[n_in + n_out :]
        in_buf, out_buf = refs[:n_in], refs[n_in : n_in + n_out]
        extra, (in_sem, out_sem) = refs[n_in + n_out : -2], refs[-2:]
        loads = [pltpu.make_async_copy(in_hbm[i], in_buf[i], in_sem.at[i]) for i in range(n_in)]
        stores = [pltpu.make_async_copy(out_buf[i], out_hbm[i], out_sem.at[i]) for i in range(n_out)]
        for load in loads:
            load.start()

        def need(*which):
            for i in which:
                loads[i].wait()

        def emit(*which):
            for i in which:
                stores[i].start()

        body(scalar_ref, in_buf, out_buf, need, emit, *extra)
        for store in stores:
            store.wait()

    held = sum(a.size * a.dtype.itemsize for a in [*ins, *outs])
    return pl.pallas_call(
        kernel,
        out_shape=outs,
        in_specs=[SMEM] + [HBM] * n_in,
        out_specs=[HBM] * n_out,
        scratch_shapes=[pltpu.VMEM(a.shape, a.dtype) for a in [*ins, *outs]]
        + list(scratch)
        + [pltpu.SemaphoreType.DMA((n_in,)), pltpu.SemaphoreType.DMA((n_out,))],
        compiler_params=pltpu.CompilerParams(vmem_limit_bytes=limit or held + (8 << 20)),
        cost_estimate=pl.CostEstimate(flops=0, bytes_accessed=0, transcendentals=0),
    )(scalars, *ins)


def run_inside(body, scalars, ins, outs, flops=0, scratch=()):
    n_in, n_out = len(ins), len(outs)
    outs = [jax.ShapeDtypeStruct(shape, dtype) for shape, dtype in outs]

    def kernel(*refs):
        body(refs[0], refs[1 : 1 + n_in], refs[1 + n_in : 1 + n_in + n_out], *refs[1 + n_in + n_out :])

    held = sum(a.size * a.dtype.itemsize for a in [*ins, *outs])
    return pl.pallas_call(
        kernel,
        out_shape=outs,
        in_specs=[SMEM] + [VMEM] * n_in,
        out_specs=[VMEM] * n_out,
        scratch_shapes=list(scratch),
        compiler_params=pltpu.CompilerParams(vmem_limit_bytes=held + (8 << 20)),
        cost_estimate=pl.CostEstimate(flops=0, bytes_accessed=0, transcendentals=0),
    )(scalars, *ins)


def one_hot(ids, n_local):
    rows = lax.broadcasted_iota(jnp.int32, (n_local, ids.shape[1]), 0)
    return (rows == ids).astype(F32).astype(BF16)


def pack_body(scalars, ins, outs, need, emit):
    features, send_rows, send_count, hub_rows = ins
    outgoing, own_hubs, chosen = outs
    n_local = features.shape[0]
    n_slots, n_dev = send_rows.shape[1], send_count.shape[1]
    capacity = n_slots // n_dev
    need(1, 2, 3)
    peer = lax.broadcasted_iota(jnp.int32, (n_dev, n_slots), 0)
    lane = lax.broadcasted_iota(jnp.int32, (n_dev, n_slots), 1)
    spread = (lane // capacity == peer).astype(F32)
    live = mul(send_count[...].astype(F32), spread)
    slot = lax.broadcasted_iota(jnp.int32, (1, n_slots), 1) % capacity
    ids = jnp.where(slot.astype(F32) < live, send_rows[...], -1)
    chosen[...] = ids
    emit(2)
    pick = one_hot(ids, n_local)
    pick_hub = one_hot(hub_rows[...], n_local)
    need(0)
    own_hubs[...] = t_mul(pick_hub, features[...]).astype(BF16)
    emit(1)
    outgoing[...] = t_mul(pick, features[...]).astype(BF16)
    emit(0)


def seed_body(side, ins, outs, need, emit, d_pre_all, aggregate):
    counts, arrived, hubs, summed, inv_deg, w_neigh, own_pre, cotangent, counts_t = ins
    hidden, d_pre, d_agg, d_pre_other, aggregate_t, d_arrived, hub_keep, hub_send = outs
    n_local, width = cotangent.shape
    n_slots = arrived.shape[0]
    n_hubs = hubs.shape[0]
    half = width // 2
    need(0, 1, 2, 3, 4)
    inv = inv_deg[...]
    for c in range(0, width, CHUNK):
        cols = slice(c, c + CHUNK)
        total = summed[:, cols] + mul(counts[:, :n_slots], arrived[:, cols])
        total = total + mul(counts[:, n_slots:], hubs[:, cols])
        mean = total * inv
        aggregate[:, cols] = mean.astype(BF16)
        aggregate_t[cols, :] = mean.T.astype(BF16)
    emit(4)
    need(5, 6, 7)
    for c in range(0, width, CHUNK):
        cols = slice(c, c + CHUNK)
        pre = own_pre[:, cols] + mul(aggregate[...], w_neigh[:, cols])
        sig = 0.5 + 0.5 * jnp.tanh(0.5 * pre)
        hidden[:, cols] = (pre * sig).astype(BF16)
        grad = cotangent[:, cols].astype(F32) * (sig * (1.0 + pre * (1.0 - sig)))
        grad = grad.astype(BF16)
        d_pre_all[:, cols] = grad
        part = slice(c % half, c % half + CHUNK)

        @pl.when(side[0] == c // half)
        def _():
            d_pre[:, part] = grad

        @pl.when(side[0] != c // half)
        def _():
            d_pre_other[:, part] = grad

    emit(3, 1, 0)
    need(8)
    for c in range(0, width, CHUNK):
        cols = slice(c, c + CHUNK)
        grad = (mul_t(d_pre_all[...], w_neigh[cols, :]) * inv).astype(BF16)
        d_agg[:, cols] = grad
        d_arrived[:, cols] = mul(counts_t[:n_slots, :], grad).astype(BF16)
        d_hubs = mul(counts_t[n_slots:, :], grad)
        part = slice(c % half, c % half + CHUNK)
        hub_keep[c // half, :, part] = d_hubs[: n_hubs // 2]
        hub_send[c // half, :, part] = d_hubs[n_hubs // 2 :].astype(BF16)
    emit(5, 7, 6, 2)


def hub_rows_of(total, k, rows):
    return jnp.concatenate([total[0, k * rows : (k + 1) * rows], total[1, k * rows : (k + 1) * rows]], 0)


def weight_body(n_part, with_hubs, mine, ins, outs, total):
    own, peer, d_own, d_peer = ins[:4]
    rows, half = outs[0].shape
    total[...] = mul(own[...], d_own[...]) + mul(peer[...], d_peer[...])
    if with_hubs:
        hubs = ins[4][...] + ins[5][...].astype(F32)
        size = hubs.shape[1] // n_part
        outs[n_part][...] = hubs[:, :size]
    for k in range(n_part):
        at = pl.ds(pl.multiple_of((mine[0] ^ k) * rows, rows), rows)
        outs[k][:rows, :] = total[at, :].astype(outs[k].dtype)
        if k > 0 and with_hubs:
            outs[k][rows:, :] = hub_rows_of(hubs, k, size).astype(BF16)


def add_up(keep, hubs, got):
    size = keep.shape[0]
    value = keep[...]
    for one in got:
        value = value + one[:size, :].astype(F32)
    if hubs is None:
        return value, None, None
    first, second = hubs[0], hubs[1]
    n_hub = first.shape[0]
    for one in got:
        tail = one[size:, :].astype(F32)
        first = first + tail[:n_hub]
        second = second + tail[n_hub:]
    return value, first, second


def halve_body(with_hubs, at_bit, where, ins, outs, total):
    hubs = ins[1] if with_hubs else None
    value, first, second = add_up(ins[0], hubs, ins[1 + int(with_hubs) :])
    total[...] = value
    keep, send = outs[:2]
    rows = keep.shape[0]
    mine = where[at_bit]
    keep[...] = total[pl.ds(pl.multiple_of(mine * rows, rows), rows), :]
    send[:rows, :] = total[pl.ds(pl.multiple_of((1 - mine) * rows, rows), rows), :].astype(BF16)
    if with_hubs:
        n_hub = first.shape[0] // 2
        outs[2][0] = first[:n_hub]
        outs[2][1] = second[:n_hub]
        send[rows:, :] = jnp.concatenate([first[n_hub:], second[n_hub:]], 0).astype(BF16)


def meet_body(with_hubs, where, ins, outs):
    hubs = ins[1] if with_hubs else None
    value, first, second = add_up(ins[0], hubs, ins[1 + int(with_hubs) :])
    rows = value.shape[0]
    outs[0][:rows, :] = value.astype(BF16)
    if with_hubs:
        n_hub = first.shape[0] // 2
        outs[1][0] = first[:n_hub]
        outs[1][1] = second[:n_hub]
        outs[0][rows:, :] = jnp.concatenate([first[n_hub:], second[n_hub:]], 0).astype(BF16)


def close_body(with_hubs, where, ins, outs):
    rows = outs[0].shape[0]
    own, got = ins[0], ins[1]
    outs[0][...] = (own[:rows, :].astype(F32) + got[:rows, :].astype(F32)).astype(BF16)
    if with_hubs:
        tail = got[rows:, :].astype(F32)
        n_hub = tail.shape[0] // 2
        outs[1][0] = ins[2][0] + tail[:n_hub]
        outs[1][1] = ins[2][1] + tail[n_hub:]


def join_body(scalars, ins, outs):
    at = 0
    for one in ins:
        outs[0][at : at + one.shape[0], :] = one[...]
        at += one.shape[0]


def node_body(side, ins, outs, need, emit):
    w_self, d_pre, d_other, counts_t, d_agg, chosen, returned, hub_rows, hub_back = ins
    (grad_x,) = outs
    n_local = d_pre.shape[0]
    width = w_self.shape[0]
    half = width // 2
    need(*range(len(ins)))
    picked = one_hot(chosen[...], n_local)
    hub_picked = one_hot(hub_rows[...], n_local)
    mine = pl.ds(pl.multiple_of(side[0] * half, half), half)
    theirs = pl.ds(pl.multiple_of((1 - side[0]) * half, half), half)
    for c in range(0, width, CHUNK):
        cols = slice(c, c + CHUNK)
        part = slice(c % half, c % half + CHUNK)
        back = hub_back[c // half, :, part]
        high = back.astype(BF16)
        low = (back - high.astype(F32)).astype(BF16)
        total = mul_t(d_pre[...], w_self[cols, mine]) + mul_t(d_other[...], w_self[cols, theirs])
        total = total + mul(counts_t[...], d_agg[:, cols])
        total = total + mul(picked, returned[:, cols])
        total = total + mul(hub_picked, high) + mul(hub_picked, low)
        grad_x[:, cols] = total.astype(BF16)
    emit(0)


def place_body(n_xy, n_z, where, ins, outs):
    half = ins[0].shape[1]
    rows = ins[0].shape[0] // n_z
    for i, block in enumerate(ins):
        core, k = divmod(i, n_xy)
        cols = pl.ds(pl.multiple_of((where[0] ^ core) * half, half), half)
        for j in range(n_z):
            at = pl.ds(pl.multiple_of(((where[1] ^ k) * n_z + (where[2] ^ j)) * rows, rows), rows)
            outs[0][at, cols] = block[j * rows : (j + 1) * rows, :]


def on_device(
    features,
    neighbours,
    degrees,
    send_rows,
    send_count,
    hub_rows,
    w_self,
    w_neigh,
    bias_term,
    cotangent,
):
    n_row = lax.axis_size("row")
    n_col = lax.axis_size("col")
    n_dev = n_row * n_col
    me = lax.axis_index("row") * n_col + lax.axis_index("col")
    n_local, width = features.shape
    fanout = neighbours.shape[1]
    n_slots = send_rows.shape[1]
    capacity = n_slots // n_dev
    n_hub = hub_rows.shape[0]
    n_hubs = n_dev * n_hub
    half = width // 2
    hub_base = n_local + n_slots
    wide = (n_local, width)

    core = n_col
    xy_bits = [1] + [n_col << i for i in range(1, n_row.bit_length() - 1)]
    z_bits = [1 << i for i in range(1, n_col.bit_length() - 1)]
    hub_bits = z_bits[::-1] + xy_bits + [core]
    n_xy, n_z = 1 << len(xy_bits), 1 << len(z_bits)

    def spread(bits, k):
        return sum(mask for i, mask in enumerate(bits) if k >> i & 1)

    def bit(mask):
        return (me & mask) // mask

    def place_of(bits):
        return sum(bit(mask) << i for i, mask in enumerate(bits))

    def swap(value, mask):
        return lax.ppermute(value, AXES, [(i, i ^ mask) for i in range(n_dev)])

    side, xy_me, z_me = bit(core), place_of(xy_bits), place_of(z_bits[-2::-1])
    z_at = jnp.stack([bit(mask) for mask in z_bits])

    hub_row = hub_rows.reshape(1, n_hub)
    outgoing, own_hubs, chosen = run(
        pack_body,
        side[None],
        [features, send_rows, send_count, hub_row],
        [((n_slots, width), BF16), ((n_hub, width), BF16), ((1, n_slots), jnp.int32)],
        flops=2 * n_slots * n_local * width,
        limit=VMEM_LIMIT,
    )
    arrived = lax.all_to_all(
        outgoing.reshape(n_dev, capacity, width), AXES, split_axis=0, concat_axis=0, tiled=True
    ).reshape(n_slots, width)

    hubs = jnp.concatenate([own_hubs] + [swap(own_hubs, spread(z_bits[::-1], k)) for k in range(1, n_z)], 0)
    for mask in xy_bits + [core]:
        hubs = jnp.concatenate([hubs, swap(hubs, mask)], 0)
    feat_t = features.T
    peer_feat_t = swap(feat_t, core)

    hub_id = neighbours - hub_base
    relative = (hub_id // n_hub) ^ me
    spot = sum(((relative & mask) // mask) << i for i, mask in enumerate(hub_bits))
    where_to = jnp.where(hub_id >= 0, hub_base + spot * n_hub + hub_id % n_hub, neighbours)
    where_to = jnp.where(jnp.arange(fanout, dtype=jnp.int32)[None, :] < degrees[:, None], where_to, -1)
    to_t = where_to.T

    def count(first, last):
        ids = jnp.arange(first, last, dtype=jnp.int32)
        found = sum((where_to[:, j : j + 1] == ids[None, :]).astype(F32) for j in range(fanout))
        found_t = sum((to_t[j : j + 1, :] == ids[:, None]).astype(F32) for j in range(fanout))
        return found.astype(BF16), found_t.astype(BF16)

    counts_own, counts_own_t = count(0, n_local)
    counts_far, counts_far_t = count(n_local, hub_base + n_hubs)
    inv_deg = 1.0 / degrees.astype(F32)[:, None]
    summed = mul(counts_own, features)
    own_pre = mul(features, w_self) + bias_term[None, :]

    hidden, d_pre, d_agg, d_other, agg_t, d_arrived, hub_keep, hub_send = run(
        seed_body,
        side[None],
        [counts_far, arrived, hubs, summed, inv_deg, w_neigh, own_pre, cotangent, counts_far_t],
        [
            (wide, BF16),
            ((n_local, half), BF16),
            (wide, BF16),
            ((n_local, half), BF16),
            ((width, n_local), BF16),
            ((n_slots, width), BF16),
            ((2, n_hubs // 2, half), F32),
            ((2, n_hubs // 2, half), BF16),
        ],
        flops=4 * n_local * width * (width + n_slots + n_hubs),
        scratch=[pltpu.VMEM(wide, BF16), pltpu.VMEM(wide, BF16)],
        limit=VMEM_LIMIT,
    )
    returned = lax.all_to_all(
        d_arrived.reshape(n_dev, capacity, width), AXES, split_axis=0, concat_axis=0, tiled=True
    ).reshape(n_slots, width)
    peer_d_pre = swap(d_other, core)
    hub_got = swap(hub_send, core)
    peer_agg_t = swap(agg_t, core)

    xy_rows = width // n_xy
    hub_xy = n_hubs // 2 // n_xy

    def across(parts, bits, first=1):
        return [swap(part, spread(bits, first + k)) for k, part in enumerate(parts)]

    def in_order(values, earlier):
        return list(lax.optimization_barrier((*values, *earlier))[: len(values)])

    def start_sum(own, peer, hub_in):
        extra = 2 * hub_xy if hub_in else 0
        return run_inside(
            functools.partial(weight_body, n_xy, bool(hub_in)),
            xy_me[None],
            [own, peer, d_pre, peer_d_pre] + hub_in,
            [((xy_rows, half), F32)]
            + [((xy_rows + extra, half), BF16)] * (n_xy - 1)
            + ([((2, hub_xy, half), F32)] if hub_in else []),
            flops=4 * width * half * n_local,
            scratch=[pltpu.VMEM((width, half), F32)],
        )

    def halve(keep, hub_in, got, at_bit):
        rows = keep.shape[0] // 2
        n_hub = hub_in[0].shape[1] // 2 if hub_in else 0
        keep, send, *hub_in = run_inside(
            functools.partial(halve_body, bool(hub_in), at_bit),
            z_at,
            [keep] + hub_in + got,
            [((rows, half), F32), ((rows + 2 * n_hub, half), BF16)] + [((2, n_hub, half), F32)] * bool(hub_in),
            scratch=[pltpu.VMEM((2 * rows, half), F32)],
        )
        return keep, hub_in, [swap(send, z_bits[at_bit])]

    def sum_line(keep, hub_in, got):
        for at_bit in range(len(z_bits) - 1):
            keep, hub_in, got = halve(keep, hub_in, got, at_bit)
        rows = keep.shape[0]
        n_hub = hub_in[0].shape[1] // 2 if hub_in else 0
        hub_out = [((2, n_hub, half), F32)] * bool(hub_in)
        own, *hub_in = run_inside(
            functools.partial(meet_body, bool(hub_in)),
            z_at,
            [keep] + hub_in + got,
            [((rows + 2 * n_hub, half), BF16)] + hub_out,
        )
        return run_inside(
            functools.partial(close_body, bool(hub_in)),
            z_at,
            [own, swap(own, z_bits[-1])] + hub_in,
            [((rows, half), BF16)] + hub_out,
        )

    def gather_line(own):
        for mask in z_bits[-2::-1]:
            pair = [own, swap(own, mask)]
            (own,) = run_inside(join_body, z_at, pair, [((2 * own.shape[0], half), BF16)])
        return own

    self_xy = start_sum(feat_t, peer_feat_t, [])
    self_got = across(self_xy[1:], xy_bits)
    agg_pair = in_order([agg_t, peer_agg_t], self_xy)
    neigh_xy = start_sum(*agg_pair, [hub_keep, hub_got])
    neigh_got = across(neigh_xy[1:n_xy], xy_bits)
    self_got = in_order(self_got, [*neigh_xy, counts_own_t])
    (self_own,) = sum_line(self_xy[0], [], self_got)
    neigh_own, hub_back = sum_line(neigh_xy[0], [neigh_xy[n_xy]], neigh_got)

    def place(blocks):
        return run_inside(
            functools.partial(place_body, n_xy, n_z // 2),
            jnp.stack([side, xy_me, z_me]),
            blocks + [swap(one, core) for one in blocks],
            [((width, width), BF16)],
        )[0]

    self_line = gather_line(self_own)
    self_blocks = [self_line] + across([self_line] * (n_xy - 1), xy_bits)
    neigh_line = gather_line(neigh_own)
    (neigh_line,) = in_order([neigh_line], self_blocks)
    neigh_blocks = [neigh_line] + across([neigh_line] * (n_xy - 1), xy_bits)
    grad_self = place(in_order(self_blocks, neigh_blocks[:1]))
    (grad_x,) = run(
        node_body,
        side[None],
        [w_self, d_pre, d_other, counts_own_t, d_agg, chosen, returned, hub_row, hub_back],
        [(wide, BF16)],
        flops=2 * n_local * width * (width + n_local + n_slots),
        limit=VMEM_LIMIT,
    )
    grad_neigh = place(in_order(neigh_blocks, [grad_x, grad_self]))
    return hidden, grad_x, grad_self, grad_neigh


def solution(mesh):
    split = P(AXES, None)
    in_specs = (split, split, P(AXES), split, split, P(AXES), P(), P(), P(), split)
    out_specs = (split, split, P(), P())
    return jax.shard_map(
        on_device, mesh=mesh, in_specs=in_specs, out_specs=out_specs, check_vma=False
    )
```

```python
import functools

import jax
import jax.numpy as jnp
from jax import lax
from jax.experimental import pallas as pl
from jax.experimental.pallas import tpu as pltpu
from jax.sharding import PartitionSpec as P

AXES = ("row", "col")
BF16 = jnp.bfloat16
F32 = jnp.float32
CHUNK = 512
HBM = pl.BlockSpec(memory_space=pl.ANY)
VMEM_LIMIT = 56 << 20
VMEM = pl.BlockSpec(memory_space=pltpu.VMEM)
SMEM = pl.BlockSpec(memory_space=pltpu.SMEM)


def mul(left, right):
    return jnp.dot(left, right, preferred_element_type=F32)


def mul_t(left, right):
    return lax.dot_general(left, right, (((1,), (1,)), ((), ())), preferred_element_type=F32)


def t_mul(left, right):
    return lax.dot_general(left, right, (((0,), (0,)), ((), ())), preferred_element_type=F32)


def run(body, scalars, ins, outs, flops=0, scratch=(), limit=0):
    n_in, n_out = len(ins), len(outs)
    outs = [jax.ShapeDtypeStruct(shape, dtype) for shape, dtype in outs]

    def kernel(*refs):
        scalar_ref, refs = refs[0], refs[1:]
        in_hbm, out_hbm = refs[:n_in], refs[n_in : n_in + n_out]
        refs = refs[n_in + n_out :]
        in_buf, out_buf = refs[:n_in], refs[n_in : n_in + n_out]
        extra, (in_sem, out_sem) = refs[n_in + n_out : -2], refs[-2:]
        loads = [pltpu.make_async_copy(in_hbm[i], in_buf[i], in_sem.at[i]) for i in range(n_in)]
        stores = [pltpu.make_async_copy(out_buf[i], out_hbm[i], out_sem.at[i]) for i in range(n_out)]
        for load in loads:
            load.start()

        def need(*which):
            for i in which:
                loads[i].wait()

        def emit(*which):
            for i in which:
                stores[i].start()

        body(scalar_ref, in_buf, out_buf, need, emit, *extra)
        for store in stores:
            store.wait()

    held = sum(a.size * a.dtype.itemsize for a in [*ins, *outs])
    return pl.pallas_call(
        kernel,
        out_shape=outs,
        in_specs=[SMEM] + [HBM] * n_in,
        out_specs=[HBM] * n_out,
        scratch_shapes=[pltpu.VMEM(a.shape, a.dtype) for a in [*ins, *outs]]
        + list(scratch)
        + [pltpu.SemaphoreType.DMA((n_in,)), pltpu.SemaphoreType.DMA((n_out,))],
        compiler_params=pltpu.CompilerParams(vmem_limit_bytes=limit or held + (8 << 20)),
        cost_estimate=pl.CostEstimate(flops=0, bytes_accessed=0, transcendentals=0),
    )(scalars, *ins)


def run_inside(body, scalars, ins, outs, flops=0, scratch=()):
    n_in, n_out = len(ins), len(outs)
    outs = [jax.ShapeDtypeStruct(shape, dtype) for shape, dtype in outs]

    def kernel(*refs):
        body(refs[0], refs[1 : 1 + n_in], refs[1 + n_in : 1 + n_in + n_out], *refs[1 + n_in + n_out :])

    held = sum(a.size * a.dtype.itemsize for a in [*ins, *outs])
    return pl.pallas_call(
        kernel,
        out_shape=outs,
        in_specs=[SMEM] + [VMEM] * n_in,
        out_specs=[VMEM] * n_out,
        scratch_shapes=list(scratch),
        compiler_params=pltpu.CompilerParams(vmem_limit_bytes=held + (8 << 20)),
        cost_estimate=pl.CostEstimate(flops=0, bytes_accessed=0, transcendentals=0),
    )(scalars, *ins)


def one_hot(ids, n_local):
    rows = lax.broadcasted_iota(jnp.int32, (n_local, ids.shape[1]), 0)
    return (rows == ids).astype(F32).astype(BF16)


def pack_body(scalars, ins, outs, need, emit):
    features, send_rows, send_count, hub_rows = ins
    outgoing, own_hubs, chosen = outs
    n_local = features.shape[0]
    n_slots, n_dev = send_rows.shape[1], send_count.shape[1]
    capacity = n_slots // n_dev
    need(1, 2, 3)
    peer = lax.broadcasted_iota(jnp.int32, (n_dev, n_slots), 0)
    lane = lax.broadcasted_iota(jnp.int32, (n_dev, n_slots), 1)
    spread = (lane // capacity == peer).astype(F32)
    live = mul(send_count[...].astype(F32), spread)
    slot = lax.broadcasted_iota(jnp.int32, (1, n_slots), 1) % capacity
    ids = jnp.where(slot.astype(F32) < live, send_rows[...], -1)
    chosen[...] = ids
    emit(2)
    pick = one_hot(ids, n_local)
    pick_hub = one_hot(hub_rows[...], n_local)
    need(0)
    own_hubs[...] = t_mul(pick_hub, features[...]).astype(BF16)
    emit(1)
    outgoing[...] = t_mul(pick, features[...]).astype(BF16)
    emit(0)


def seed_body(side, ins, outs, need, emit, d_pre_all, aggregate):
    counts, arrived, hubs, summed, inv_deg, w_neigh, own_pre, cotangent, counts_t = ins
    hidden, d_pre, d_agg, d_pre_other, aggregate_t, d_arrived, hub_keep, hub_send = outs
    n_local, width = cotangent.shape
    n_slots = arrived.shape[0]
    n_hubs = hubs.shape[0]
    half = width // 2
    need(0, 1, 2, 3, 4)
    inv = inv_deg[...]
    for c in range(0, width, CHUNK):
        cols = slice(c, c + CHUNK)
        total = summed[:, cols] + mul(counts[:, :n_slots], arrived[:, cols])
        total = total + mul(counts[:, n_slots:], hubs[:, cols])
        mean = total * inv
        aggregate[:, cols] = mean.astype(BF16)
        aggregate_t[cols, :] = mean.T.astype(BF16)
    emit(4)
    need(5, 6, 7)
    for c in range(0, width, CHUNK):
        cols = slice(c, c + CHUNK)
        pre = own_pre[:, cols] + mul(aggregate[...], w_neigh[:, cols])
        sig = 0.5 + 0.5 * jnp.tanh(0.5 * pre)
        hidden[:, cols] = (pre * sig).astype(BF16)
        grad = cotangent[:, cols].astype(F32) * (sig * (1.0 + pre * (1.0 - sig)))
        grad = grad.astype(BF16)
        d_pre_all[:, cols] = grad
        part = slice(c % half, c % half + CHUNK)

        @pl.when(side[0] == c // half)
        def _():
            d_pre[:, part] = grad

        @pl.when(side[0] != c // half)
        def _():
            d_pre_other[:, part] = grad

    emit(3, 1, 0)
    need(8)
    for c in range(0, width, CHUNK):
        cols = slice(c, c + CHUNK)
        grad = (mul_t(d_pre_all[...], w_neigh[cols, :]) * inv).astype(BF16)
        d_agg[:, cols] = grad
        d_arrived[:, cols] = mul(counts_t[:n_slots, :], grad).astype(BF16)
        d_hubs = mul(counts_t[n_slots:, :], grad)
        part = slice(c % half, c % half + CHUNK)
        hub_keep[c // half, :, part] = d_hubs[: n_hubs // 2]
        hub_send[c // half, :, part] = d_hubs[n_hubs // 2 :].astype(BF16)
    emit(5, 7, 6, 2)


def hub_rows_of(total, k, rows):
    return jnp.concatenate([total[0, k * rows : (k + 1) * rows], total[1, k * rows : (k + 1) * rows]], 0)


def weight_body(n_part, with_hubs, mine, ins, outs, total):
    own, peer, d_own, d_peer = ins[:4]
    rows, half = outs[0].shape
    total[...] = mul(own[...], d_own[...]) + mul(peer[...], d_peer[...])
    if with_hubs:
        hubs = ins[4][...] + ins[5][...].astype(F32)
        size = hubs.shape[1] // n_part
        outs[n_part][...] = hubs[:, :size]
    for k in range(n_part):
        at = pl.ds(pl.multiple_of((mine[0] ^ k) * rows, rows), rows)
        outs[k][:rows, :] = total[at, :].astype(outs[k].dtype)
        if k > 0 and with_hubs:
            outs[k][rows:, :] = hub_rows_of(hubs, k, size).astype(BF16)


def add_up(keep, hubs, got):
    size = keep.shape[0]
    value = keep[...]
    for one in got:
        value = value + one[:size, :].astype(F32)
    if hubs is None:
        return value, None, None
    first, second = hubs[0], hubs[1]
    n_hub = first.shape[0]
    for one in got:
        tail = one[size:, :].astype(F32)
        first = first + tail[:n_hub]
        second = second + tail[n_hub:]
    return value, first, second


def halve_body(with_hubs, at_bit, where, ins, outs, total):
    hubs = ins[1] if with_hubs else None
    value, first, second = add_up(ins[0], hubs, ins[1 + int(with_hubs) :])
    total[...] = value
    keep, send = outs[:2]
    rows = keep.shape[0]
    mine = where[at_bit]
    keep[...] = total[pl.ds(pl.multiple_of(mine * rows, rows), rows), :]
    send[:rows, :] = total[pl.ds(pl.multiple_of((1 - mine) * rows, rows), rows), :].astype(BF16)
    if with_hubs:
        n_hub = first.shape[0] // 2
        outs[2][0] = first[:n_hub]
        outs[2][1] = second[:n_hub]
        send[rows:, :] = jnp.concatenate([first[n_hub:], second[n_hub:]], 0).astype(BF16)


def meet_body(with_hubs, where, ins, outs):
    hubs = ins[1] if with_hubs else None
    value, first, second = add_up(ins[0], hubs, ins[1 + int(with_hubs) :])
    rows = value.shape[0]
    outs[0][:rows, :] = value.astype(BF16)
    if with_hubs:
        n_hub = first.shape[0] // 2
        outs[1][0] = first[:n_hub]
        outs[1][1] = second[:n_hub]
        outs[0][rows:, :] = jnp.concatenate([first[n_hub:], second[n_hub:]], 0).astype(BF16)


def close_body(with_hubs, where, ins, outs):
    rows = outs[0].shape[0]
    own, got = ins[0], ins[1]
    outs[0][...] = (own[:rows, :].astype(F32) + got[:rows, :].astype(F32)).astype(BF16)
    if with_hubs:
        tail = got[rows:, :].astype(F32)
        n_hub = tail.shape[0] // 2
        outs[1][0] = ins[2][0] + tail[:n_hub]
        outs[1][1] = ins[2][1] + tail[n_hub:]


def join_body(scalars, ins, outs):
    at = 0
    for one in ins:
        outs[0][at : at + one.shape[0], :] = one[...]
        at += one.shape[0]


def node_body(side, ins, outs, need, emit):
    w_self, d_pre, d_other, counts_t, d_agg, chosen, returned, hub_rows, hub_back = ins
    (grad_x,) = outs
    n_local = d_pre.shape[0]
    width = w_self.shape[0]
    half = width // 2
    need(*range(len(ins)))
    picked = one_hot(chosen[...], n_local)
    hub_picked = one_hot(hub_rows[...], n_local)
    mine = pl.ds(pl.multiple_of(side[0] * half, half), half)
    theirs = pl.ds(pl.multiple_of((1 - side[0]) * half, half), half)
    for c in range(0, width, CHUNK):
        cols = slice(c, c + CHUNK)
        part = slice(c % half, c % half + CHUNK)
        back = hub_back[c // half, :, part]
        high = back.astype(BF16)
        low = (back - high.astype(F32)).astype(BF16)
        total = mul_t(d_pre[...], w_self[cols, mine]) + mul_t(d_other[...], w_self[cols, theirs])
        total = total + mul(counts_t[...], d_agg[:, cols])
        total = total + mul(picked, returned[:, cols])
        total = total + mul(hub_picked, high) + mul(hub_picked, low)
        grad_x[:, cols] = total.astype(BF16)
    emit(0)


def place_body(n_xy, n_z, where, ins, outs):
    half = ins[0].shape[1]
    rows = ins[0].shape[0] // n_z
    for i, block in enumerate(ins):
        core, at = divmod(i, n_xy)
        k = (n_xy - at) % n_xy
        cols = pl.ds(pl.multiple_of((where[0] ^ core) * half, half), half)
        for j in range(n_z):
            at = pl.ds(pl.multiple_of(((where[1] ^ k) * n_z + (where[2] ^ j)) * rows, rows), rows)
            outs[0][at, cols] = block[j * rows : (j + 1) * rows, :]


def on_device(
    features,
    neighbours,
    degrees,
    send_rows,
    send_count,
    hub_rows,
    w_self,
    w_neigh,
    bias_term,
    cotangent,
):
    n_row = lax.axis_size("row")
    n_col = lax.axis_size("col")
    n_dev = n_row * n_col
    me = lax.axis_index("row") * n_col + lax.axis_index("col")
    n_local, width = features.shape
    fanout = neighbours.shape[1]
    n_slots = send_rows.shape[1]
    capacity = n_slots // n_dev
    n_hub = hub_rows.shape[0]
    n_hubs = n_dev * n_hub
    half = width // 2
    hub_base = n_local + n_slots
    wide = (n_local, width)

    core = n_col
    xy_bits = [1] + [n_col << i for i in range(1, n_row.bit_length() - 1)]
    z_bits = [1 << i for i in range(1, n_col.bit_length() - 1)]
    hub_bits = z_bits[::-1] + xy_bits + [core]
    n_xy, n_z = 1 << len(xy_bits), 1 << len(z_bits)

    def spread(bits, k):
        return sum(mask for i, mask in enumerate(bits) if k >> i & 1)

    def bit(mask):
        return (me & mask) // mask

    def place_of(bits):
        return sum(bit(mask) << i for i, mask in enumerate(bits))

    def swap(value, mask):
        return lax.ppermute(value, AXES, [(i, i ^ mask) for i in range(n_dev)])

    side, xy_me, z_me = bit(core), place_of(xy_bits), place_of(z_bits[-2::-1])
    z_at = jnp.stack([bit(mask) for mask in z_bits])

    hub_row = hub_rows.reshape(1, n_hub)
    outgoing, own_hubs, chosen = run(
        pack_body,
        side[None],
        [features, send_rows, send_count, hub_row],
        [((n_slots, width), BF16), ((n_hub, width), BF16), ((1, n_slots), jnp.int32)],
        flops=2 * n_slots * n_local * width,
        limit=VMEM_LIMIT,
    )
    arrived = lax.all_to_all(
        outgoing.reshape(n_dev, capacity, width), AXES, split_axis=0, concat_axis=0, tiled=True
    ).reshape(n_slots, width)

    hubs = jnp.concatenate([own_hubs] + [swap(own_hubs, spread(z_bits[::-1], k)) for k in range(1, n_z)], 0)
    for mask in xy_bits + [core]:
        hubs = jnp.concatenate([hubs, swap(hubs, mask)], 0)
    feat_t = features.T
    peer_feat_t = swap(feat_t, core)

    hub_id = neighbours - hub_base
    relative = (hub_id // n_hub) ^ me
    spot = sum(((relative & mask) // mask) << i for i, mask in enumerate(hub_bits))
    where_to = jnp.where(hub_id >= 0, hub_base + spot * n_hub + hub_id % n_hub, neighbours)
    where_to = jnp.where(jnp.arange(fanout, dtype=jnp.int32)[None, :] < degrees[:, None], where_to, -1)
    to_t = where_to.T

    def count(first, last):
        ids = jnp.arange(first, last, dtype=jnp.int32)
        found = sum((where_to[:, j : j + 1] == ids[None, :]).astype(F32) for j in range(fanout))
        found_t = sum((to_t[j : j + 1, :] == ids[:, None]).astype(F32) for j in range(fanout))
        return found.astype(BF16), found_t.astype(BF16)

    counts_own, counts_own_t = count(0, n_local)
    counts_far, counts_far_t = count(n_local, hub_base + n_hubs)
    inv_deg = 1.0 / degrees.astype(F32)[:, None]
    summed = mul(counts_own, features)
    own_pre = mul(features, w_self) + bias_term[None, :]

    hidden, d_pre, d_agg, d_other, agg_t, d_arrived, hub_keep, hub_send = run(
        seed_body,
        side[None],
        [counts_far, arrived, hubs, summed, inv_deg, w_neigh, own_pre, cotangent, counts_far_t],
        [
            (wide, BF16),
            ((n_local, half), BF16),
            (wide, BF16),
            ((n_local, half), BF16),
            ((width, n_local), BF16),
            ((n_slots, width), BF16),
            ((2, n_hubs // 2, half), F32),
            ((2, n_hubs // 2, half), BF16),
        ],
        flops=4 * n_local * width * (width + n_slots + n_hubs),
        scratch=[pltpu.VMEM(wide, BF16), pltpu.VMEM(wide, BF16)],
        limit=VMEM_LIMIT,
    )
    returned = lax.all_to_all(
        d_arrived.reshape(n_dev, capacity, width), AXES, split_axis=0, concat_axis=0, tiled=True
    ).reshape(n_slots, width)
    peer_d_pre = swap(d_other, core)
    hub_got = swap(hub_send, core)
    peer_agg_t = swap(agg_t, core)

    xy_rows = width // n_xy
    hub_xy = n_hubs // 2 // n_xy

    def across(parts, bits):
        return [swap(parts[k - 1], spread(bits, k)) for k in range(len(parts), 0, -1)]

    def in_order(values, earlier):
        return list(lax.optimization_barrier((*values, *earlier))[: len(values)])

    def start_sum(own, peer, hub_in):
        extra = 2 * hub_xy if hub_in else 0
        return run_inside(
            functools.partial(weight_body, n_xy, bool(hub_in)),
            xy_me[None],
            [own, peer, d_pre, peer_d_pre] + hub_in,
            [((xy_rows, half), F32)]
            + [((xy_rows + extra, half), BF16)] * (n_xy - 1)
            + ([((2, hub_xy, half), F32)] if hub_in else []),
            flops=4 * width * half * n_local,
            scratch=[pltpu.VMEM((width, half), F32)],
        )

    def halve(keep, hub_in, got, at_bit):
        rows = keep.shape[0] // 2
        n_hub = hub_in[0].shape[1] // 2 if hub_in else 0
        keep, send, *hub_in = run_inside(
            functools.partial(halve_body, bool(hub_in), at_bit),
            z_at,
            [keep] + hub_in + got,
            [((rows, half), F32), ((rows + 2 * n_hub, half), BF16)] + [((2, n_hub, half), F32)] * bool(hub_in),
            scratch=[pltpu.VMEM((2 * rows, half), F32)],
        )
        return keep, hub_in, [swap(send, z_bits[at_bit])]

    def sum_line(keep, hub_in, got):
        for at_bit in range(len(z_bits) - 1):
            keep, hub_in, got = halve(keep, hub_in, got, at_bit)
        rows = keep.shape[0]
        n_hub = hub_in[0].shape[1] // 2 if hub_in else 0
        hub_out = [((2, n_hub, half), F32)] * bool(hub_in)
        own, *hub_in = run_inside(
            functools.partial(meet_body, bool(hub_in)),
            z_at,
            [keep] + hub_in + got,
            [((rows + 2 * n_hub, half), BF16)] + hub_out,
        )
        return run_inside(
            functools.partial(close_body, bool(hub_in)),
            z_at,
            [own, swap(own, z_bits[-1])] + hub_in,
            [((rows, half), BF16)] + hub_out,
        )

    def gather_line(own):
        for mask in z_bits[-2::-1]:
            pair = [own, swap(own, mask)]
            (own,) = run_inside(join_body, z_at, pair, [((2 * own.shape[0], half), BF16)])
        return own

    self_xy = start_sum(feat_t, peer_feat_t, [])
    self_got = across(self_xy[1:], xy_bits)
    agg_pair = in_order([agg_t, peer_agg_t], self_xy)
    neigh_xy = start_sum(*agg_pair, [hub_keep, hub_got])
    neigh_got = across(neigh_xy[1:n_xy], xy_bits)
    self_got = in_order(self_got, [*neigh_xy, counts_own_t])
    (self_own,) = sum_line(self_xy[0], [], self_got)
    neigh_own, hub_back = sum_line(neigh_xy[0], [neigh_xy[n_xy]], neigh_got)

    def place(blocks):
        return run_inside(
            functools.partial(place_body, n_xy, n_z // 2),
            jnp.stack([side, xy_me, z_me]),
            blocks + [swap(one, core) for one in blocks],
            [((width, width), BF16)],
        )[0]

    self_line = gather_line(self_own)
    self_blocks = [self_line] + across([self_line] * (n_xy - 1), xy_bits)
    neigh_line = gather_line(neigh_own)
    (neigh_line,) = in_order([neigh_line], self_blocks)
    neigh_blocks = [neigh_line] + across([neigh_line] * (n_xy - 1), xy_bits)
    grad_self = place(in_order(self_blocks, neigh_blocks[:1]))
    (grad_x,) = run(
        node_body,
        side[None],
        [w_self, d_pre, d_other, counts_own_t, d_agg, chosen, returned, hub_row, hub_back],
        [(wide, BF16)],
        flops=2 * n_local * width * (width + n_local + n_slots),
        limit=VMEM_LIMIT,
    )
    grad_neigh = place(in_order(neigh_blocks, [grad_x, grad_self]))
    return hidden, grad_x, grad_self, grad_neigh


def solution(mesh):
    split = P(AXES, None)
    in_specs = (split, split, P(AXES), split, split, P(AXES), P(), P(), P(), split)
    out_specs = (split, split, P(), P())
    return jax.shard_map(
        on_device, mesh=mesh, in_specs=in_specs, out_specs=out_specs, check_vma=False
    )
```

```python
import functools

import jax
import jax.numpy as jnp
from jax import lax
from jax.experimental import pallas as pl
from jax.experimental.pallas import tpu as pltpu
from jax.sharding import PartitionSpec as P

AXES = ("row", "col")
BF16 = jnp.bfloat16
F32 = jnp.float32
CHUNK = 512
HBM = pl.BlockSpec(memory_space=pl.ANY)
VMEM_LIMIT = 56 << 20
VMEM = pl.BlockSpec(memory_space=pltpu.VMEM)
SMEM = pl.BlockSpec(memory_space=pltpu.SMEM)


def mul(left, right):
    return jnp.dot(left, right, preferred_element_type=F32)


def mul_t(left, right):
    return lax.dot_general(left, right, (((1,), (1,)), ((), ())), preferred_element_type=F32)


def t_mul(left, right):
    return lax.dot_general(left, right, (((0,), (0,)), ((), ())), preferred_element_type=F32)


def run(body, scalars, ins, outs, flops=0, scratch=(), limit=0, halved=()):
    n_in, n_out = len(ins), len(outs)
    outs = [jax.ShapeDtypeStruct(shape, dtype) for shape, dtype in outs]

    def kernel(*refs):
        scalar_ref, refs = refs[0], refs[1:]
        in_hbm, out_hbm = refs[:n_in], refs[n_in : n_in + n_out]
        refs = refs[n_in + n_out :]
        in_buf, out_buf = refs[:n_in], refs[n_in : n_in + n_out]
        extra, (in_sem, out_sem) = refs[n_in + n_out : -2], refs[-2:]
        loads = [pltpu.make_async_copy(in_hbm[i], in_buf[i], in_sem.at[i]) for i in range(n_in)]
        stores = {}
        for i in range(n_out):
            cut = out_buf[i].shape[-1] // 2
            if i in halved:
                for part in range(2):
                    cols = slice(part * cut, (part + 1) * cut)
                    stores[i, part] = pltpu.make_async_copy(
                        out_buf[i].at[:, cols], out_hbm[i].at[:, cols], out_sem.at[i + part * n_out]
                    )
            else:
                stores[i] = pltpu.make_async_copy(out_buf[i], out_hbm[i], out_sem.at[i])
        for load in loads:
            load.start()

        def need(*which):
            for i in which:
                loads[i].wait()

        def emit(*which):
            for i in which:
                stores[i].start()

        body(scalar_ref, in_buf, out_buf, need, emit, *extra)
        for store in stores.values():
            store.wait()

    held = sum(a.size * a.dtype.itemsize for a in [*ins, *outs])
    return pl.pallas_call(
        kernel,
        out_shape=outs,
        in_specs=[SMEM] + [HBM] * n_in,
        out_specs=[HBM] * n_out,
        scratch_shapes=[pltpu.VMEM(a.shape, a.dtype) for a in [*ins, *outs]]
        + list(scratch)
        + [pltpu.SemaphoreType.DMA((n_in,)), pltpu.SemaphoreType.DMA((2 * n_out,))],
        compiler_params=pltpu.CompilerParams(vmem_limit_bytes=limit or held + (8 << 20)),
        cost_estimate=pl.CostEstimate(flops=0, bytes_accessed=0, transcendentals=0),
    )(scalars, *ins)


def run_inside(body, scalars, ins, outs, flops=0, scratch=()):
    n_in, n_out = len(ins), len(outs)
    outs = [jax.ShapeDtypeStruct(shape, dtype) for shape, dtype in outs]

    def kernel(*refs):
        body(refs[0], refs[1 : 1 + n_in], refs[1 + n_in : 1 + n_in + n_out], *refs[1 + n_in + n_out :])

    held = sum(a.size * a.dtype.itemsize for a in [*ins, *outs])
    return pl.pallas_call(
        kernel,
        out_shape=outs,
        in_specs=[SMEM] + [VMEM] * n_in,
        out_specs=[VMEM] * n_out,
        scratch_shapes=list(scratch),
        compiler_params=pltpu.CompilerParams(vmem_limit_bytes=held + (3 << 20)),
        cost_estimate=pl.CostEstimate(flops=0, bytes_accessed=0, transcendentals=0),
    )(scalars, *ins)


def one_hot(ids, n_local):
    rows = lax.broadcasted_iota(jnp.int32, (n_local, ids.shape[1]), 0)
    return (rows == ids).astype(F32).astype(BF16)


def pack_body(scalars, ins, outs, need, emit):
    features, send_rows, send_count, hub_rows = ins
    outgoing, own_hubs, chosen = outs
    n_local = features.shape[0]
    n_slots, n_dev = send_rows.shape[1], send_count.shape[1]
    capacity = n_slots // n_dev
    need(1, 2, 3)
    peer = lax.broadcasted_iota(jnp.int32, (n_dev, n_slots), 0)
    lane = lax.broadcasted_iota(jnp.int32, (n_dev, n_slots), 1)
    spread = (lane // capacity == peer).astype(F32)
    live = mul(send_count[...].astype(F32), spread)
    slot = lax.broadcasted_iota(jnp.int32, (1, n_slots), 1) % capacity
    ids = jnp.where(slot.astype(F32) < live, send_rows[...], -1)
    chosen[...] = ids
    emit(2)
    pick = one_hot(ids, n_local)
    pick_hub = one_hot(hub_rows[...], n_local)
    need(0)
    own_hubs[...] = t_mul(pick_hub, features[...]).astype(BF16)
    emit(1)
    outgoing[...] = t_mul(pick, features[...]).astype(BF16)
    emit(0)


def seed_body(side, ins, outs, need, emit, d_pre_all, aggregate):
    counts, arrived, hubs, counts_own, features, inv_deg, w_neigh, own_pre, cotangent, counts_t = ins
    hidden, d_pre, d_agg, d_pre_other, aggregate_t, d_arrived, hub_keep, hub_send = outs
    n_local, width = cotangent.shape
    n_slots = arrived.shape[0]
    n_hubs = hubs.shape[0]
    half = width // 2
    need(3, 4, 0, 1, 2, 5)
    inv = inv_deg[...]
    for c in range(0, width, CHUNK):
        cols = slice(c, c + CHUNK)
        total = mul(counts_own[...], features[:, cols]) + mul(counts[:, :n_slots], arrived[:, cols])
        total = total + mul(counts[:, n_slots:], hubs[:, cols])
        mean = total * inv
        aggregate[:, cols] = mean.astype(BF16)
        aggregate_t[cols, :] = mean.T.astype(BF16)
    emit(4)
    need(6, 7, 8)
    for c in range(0, width, CHUNK):
        cols = slice(c, c + CHUNK)
        pre = own_pre[:, cols] + mul(aggregate[...], w_neigh[:, cols])
        sig = 0.5 + 0.5 * jnp.tanh(0.5 * pre)
        hidden[:, cols] = (pre * sig).astype(BF16)
        grad = cotangent[:, cols].astype(F32) * (sig * (1.0 + pre * (1.0 - sig)))
        grad = grad.astype(BF16)
        d_pre_all[:, cols] = grad
        part = slice(c % half, c % half + CHUNK)

        @pl.when(side[0] == c // half)
        def _():
            d_pre[:, part] = grad

        @pl.when(side[0] != c // half)
        def _():
            d_pre_other[:, part] = grad

    emit(3, 1, 0)
    need(9)
    for c in range(0, width, CHUNK):
        cols = slice(c, c + CHUNK)
        grad = (mul_t(d_pre_all[...], w_neigh[cols, :]) * inv).astype(BF16)
        d_agg[:, cols] = grad
        d_arrived[:, cols] = mul(counts_t[:n_slots, :], grad).astype(BF16)
        d_hubs = mul(counts_t[n_slots:, :], grad)
        part = slice(c % half, c % half + CHUNK)
        hub_keep[c // half, :, part] = d_hubs[: n_hubs // 2]
        hub_send[c // half, :, part] = d_hubs[n_hubs // 2 :].astype(BF16)
        if c + CHUNK == half or c + CHUNK == width:
            emit((5, c // half), (2, c // half))
    emit(7, 6)


def hub_rows_of(total, k, rows):
    return jnp.concatenate([total[0, k * rows : (k + 1) * rows], total[1, k * rows : (k + 1) * rows]], 0)


def weight_body(n_part, with_hubs, mine, ins, outs, total):
    own, peer, d_own, d_peer = ins[:4]
    rows, half = outs[0].shape
    total[...] = mul(own[...], d_own[...]) + mul(peer[...], d_peer[...])
    if with_hubs:
        hubs = ins[4][...] + ins[5][...].astype(F32)
        size = hubs.shape[1] // n_part
        outs[n_part][...] = hubs[:, :size]
    for k in range(n_part):
        at = pl.ds(pl.multiple_of((mine[0] ^ k) * rows, rows), rows)
        outs[k][:rows, :] = total[at, :].astype(outs[k].dtype)
        if k > 0 and with_hubs:
            outs[k][rows:, :] = hub_rows_of(hubs, k, size).astype(BF16)


def add_up(keep, hubs, got):
    size = keep.shape[0]
    value = keep[...]
    for one in got:
        value = value + one[:size, :].astype(F32)
    if hubs is None:
        return value, None, None
    first, second = hubs[0], hubs[1]
    n_hub = first.shape[0]
    for one in got:
        tail = one[size:, :].astype(F32)
        first = first + tail[:n_hub]
        second = second + tail[n_hub:]
    return value, first, second


def halve_body(with_hubs, at_bit, where, ins, outs, total):
    hubs = ins[1] if with_hubs else None
    value, first, second = add_up(ins[0], hubs, ins[1 + int(with_hubs) :])
    total[...] = value
    keep, send = outs[:2]
    rows = keep.shape[0]
    mine = where[at_bit]
    keep[...] = total[pl.ds(pl.multiple_of(mine * rows, rows), rows), :]
    send[:rows, :] = total[pl.ds(pl.multiple_of((1 - mine) * rows, rows), rows), :].astype(BF16)
    if with_hubs:
        n_hub = first.shape[0] // 2
        outs[2][0] = first[:n_hub]
        outs[2][1] = second[:n_hub]
        send[rows:, :] = jnp.concatenate([first[n_hub:], second[n_hub:]], 0).astype(BF16)


def meet_body(with_hubs, where, ins, outs):
    hubs = ins[1] if with_hubs else None
    value, first, second = add_up(ins[0], hubs, ins[1 + int(with_hubs) :])
    rows = value.shape[0]
    outs[0][:rows, :] = value.astype(BF16)
    if with_hubs:
        n_hub = first.shape[0] // 2
        outs[1][0] = first[:n_hub]
        outs[1][1] = second[:n_hub]
        outs[0][rows:, :] = jnp.concatenate([first[n_hub:], second[n_hub:]], 0).astype(BF16)


def close_body(with_hubs, where, ins, outs):
    rows = outs[0].shape[0]
    own, got = ins[0], ins[1]
    outs[0][...] = (own[:rows, :].astype(F32) + got[:rows, :].astype(F32)).astype(BF16)
    if with_hubs:
        tail = got[rows:, :].astype(F32)
        n_hub = tail.shape[0] // 2
        outs[1][0] = ins[2][0] + tail[:n_hub]
        outs[1][1] = ins[2][1] + tail[n_hub:]


def join_body(scalars, ins, outs):
    at = 0
    for one in ins:
        outs[0][at : at + one.shape[0], :] = one[...]
        at += one.shape[0]


def node_body(side, ins, outs, need, emit):
    w_self, d_pre, d_other, counts_t, d_agg, chosen, returned, hub_rows, hub_back = ins
    (grad_x,) = outs
    n_local = d_pre.shape[0]
    width = w_self.shape[0]
    half = width // 2
    need(*range(len(ins)))
    picked = one_hot(chosen[...], n_local)
    hub_picked = one_hot(hub_rows[...], n_local)
    mine = pl.ds(pl.multiple_of(side[0] * half, half), half)
    theirs = pl.ds(pl.multiple_of((1 - side[0]) * half, half), half)
    for c in range(0, width, CHUNK):
        cols = slice(c, c + CHUNK)
        part = slice(c % half, c % half + CHUNK)
        back = hub_back[c // half, :, part]
        high = back.astype(BF16)
        low = (back - high.astype(F32)).astype(BF16)
        total = mul_t(d_pre[...], w_self[cols, mine]) + mul_t(d_other[...], w_self[cols, theirs])
        total = total + mul(counts_t[...], d_agg[:, cols])
        total = total + mul(picked, returned[:, cols])
        total = total + mul(hub_picked, high) + mul(hub_picked, low)
        grad_x[:, cols] = total.astype(BF16)
    emit(0)


def place_body(n_xy, n_z, where, ins, outs):
    half = ins[0].shape[1]
    rows = ins[0].shape[0] // n_z
    for i, block in enumerate(ins):
        core, at = divmod(i, n_xy)
        k = (n_xy - at) % n_xy
        cols = pl.ds(pl.multiple_of((where[0] ^ core) * half, half), half)
        for j in range(n_z):
            at = pl.ds(pl.multiple_of(((where[1] ^ k) * n_z + (where[2] ^ j)) * rows, rows), rows)
            outs[0][at, cols] = block[j * rows : (j + 1) * rows, :]


def on_device(
    features,
    neighbours,
    degrees,
    send_rows,
    send_count,
    hub_rows,
    w_self,
    w_neigh,
    bias_term,
    cotangent,
):
    n_row = lax.axis_size("row")
    n_col = lax.axis_size("col")
    n_dev = n_row * n_col
    me = lax.axis_index("row") * n_col + lax.axis_index("col")
    n_local, width = features.shape
    fanout = neighbours.shape[1]
    n_slots = send_rows.shape[1]
    capacity = n_slots // n_dev
    n_hub = hub_rows.shape[0]
    n_hubs = n_dev * n_hub
    half = width // 2
    hub_base = n_local + n_slots
    wide = (n_local, width)

    core = n_col
    xy_bits = [1] + [n_col << i for i in range(1, n_row.bit_length() - 1)]
    z_bits = [1 << i for i in range(1, n_col.bit_length() - 1)]
    hub_bits = z_bits[::-1] + xy_bits + [core]
    n_xy, n_z = 1 << len(xy_bits), 1 << len(z_bits)

    def spread(bits, k):
        return sum(mask for i, mask in enumerate(bits) if k >> i & 1)

    def bit(mask):
        return (me & mask) // mask

    def place_of(bits):
        return sum(bit(mask) << i for i, mask in enumerate(bits))

    def swap(value, mask):
        return lax.ppermute(value, AXES, [(i, i ^ mask) for i in range(n_dev)])

    side, xy_me, z_me = bit(core), place_of(xy_bits), place_of(z_bits[-2::-1])
    z_at = jnp.stack([bit(mask) for mask in z_bits])

    hub_row = hub_rows.reshape(1, n_hub)
    outgoing, own_hubs, chosen = run(
        pack_body,
        side[None],
        [features, send_rows, send_count, hub_row],
        [((n_slots, width), BF16), ((n_hub, width), BF16), ((1, n_slots), jnp.int32)],
        flops=2 * n_slots * n_local * width,
        limit=VMEM_LIMIT,
    )
    arrived = lax.all_to_all(
        outgoing.reshape(n_dev, capacity, width), AXES, split_axis=0, concat_axis=0, tiled=True
    ).reshape(n_slots, width)

    along = [swap(own_hubs, spread(z_bits[::-1], k)) for k in range(n_z - 1, 0, -1)]
    hubs = jnp.concatenate([own_hubs] + along[::-1], 0)
    for mask in xy_bits + [core]:
        hubs = jnp.concatenate([hubs, swap(hubs, mask)], 0)
    feat_t = features.T
    peer_feat_t = swap(feat_t, core)

    hub_id = neighbours - hub_base
    relative = (hub_id // n_hub) ^ me
    spot = sum(((relative & mask) // mask) << i for i, mask in enumerate(hub_bits))
    where_to = jnp.where(hub_id >= 0, hub_base + spot * n_hub + hub_id % n_hub, neighbours)
    where_to = jnp.where(jnp.arange(fanout, dtype=jnp.int32)[None, :] < degrees[:, None], where_to, -1)
    to_t = where_to.T

    def count(first, last):
        ids = jnp.arange(first, last, dtype=jnp.int32)
        found = sum((where_to[:, j : j + 1] == ids[None, :]).astype(F32) for j in range(fanout))
        found_t = sum((to_t[j : j + 1, :] == ids[:, None]).astype(F32) for j in range(fanout))
        return found.astype(BF16), found_t.astype(BF16)

    counts_own, counts_own_t = count(0, n_local)
    counts_far, counts_far_t = count(n_local, hub_base + n_hubs)
    inv_deg = 1.0 / degrees.astype(F32)[:, None]
    own_pre = mul(features, w_self) + bias_term[None, :]

    hidden, d_pre, d_agg, d_other, agg_t, d_arrived, hub_keep, hub_send = run(
        seed_body,
        side[None],
        [counts_far, arrived, hubs, counts_own, features, inv_deg, w_neigh, own_pre, cotangent, counts_far_t],
        [
            (wide, BF16),
            ((n_local, half), BF16),
            (wide, BF16),
            ((n_local, half), BF16),
            ((width, n_local), BF16),
            ((n_slots, width), BF16),
            ((2, n_hubs // 2, half), F32),
            ((2, n_hubs // 2, half), BF16),
        ],
        flops=4 * n_local * width * (width + n_slots + n_hubs),
        scratch=[pltpu.VMEM(wide, BF16), pltpu.VMEM(wide, BF16)],
        limit=VMEM_LIMIT,
        halved=(2, 5),
    )
    returned = lax.all_to_all(
        d_arrived.reshape(n_dev, capacity, width), AXES, split_axis=0, concat_axis=0, tiled=True
    ).reshape(n_slots, width)
    peer_d_pre = swap(d_other, core)
    hub_got = swap(hub_send, core)
    peer_agg_t = swap(agg_t, core)

    xy_rows = width // n_xy
    hub_xy = n_hubs // 2 // n_xy

    def across(parts, bits):
        return [swap(parts[k - 1], spread(bits, k)) for k in range(len(parts), 0, -1)]

    def in_order(values, earlier):
        return list(lax.optimization_barrier((*values, *earlier))[: len(values)])

    def start_sum(own, peer, hub_in):
        extra = 2 * hub_xy if hub_in else 0
        return run_inside(
            functools.partial(weight_body, n_xy, bool(hub_in)),
            xy_me[None],
            [own, peer, d_pre, peer_d_pre] + hub_in,
            [((xy_rows, half), F32)]
            + [((xy_rows + extra, half), BF16)] * (n_xy - 1)
            + ([((2, hub_xy, half), F32)] if hub_in else []),
            flops=4 * width * half * n_local,
            scratch=[pltpu.VMEM((width, half), F32)],
        )

    def halve(keep, hub_in, got, at_bit):
        rows = keep.shape[0] // 2
        n_hub = hub_in[0].shape[1] // 2 if hub_in else 0
        keep, send, *hub_in = run_inside(
            functools.partial(halve_body, bool(hub_in), at_bit),
            z_at,
            [keep] + hub_in + got,
            [((rows, half), F32), ((rows + 2 * n_hub, half), BF16)] + [((2, n_hub, half), F32)] * bool(hub_in),
            scratch=[pltpu.VMEM((2 * rows, half), F32)],
        )
        return keep, hub_in, [swap(send, z_bits[at_bit])]

    def sum_line(keep, hub_in, got):
        for at_bit in range(len(z_bits) - 1):
            keep, hub_in, got = halve(keep, hub_in, got, at_bit)
        rows = keep.shape[0]
        n_hub = hub_in[0].shape[1] // 2 if hub_in else 0
        hub_out = [((2, n_hub, half), F32)] * bool(hub_in)
        own, *hub_in = run_inside(
            functools.partial(meet_body, bool(hub_in)),
            z_at,
            [keep] + hub_in + got,
            [((rows + 2 * n_hub, half), BF16)] + hub_out,
        )
        return run_inside(
            functools.partial(close_body, bool(hub_in)),
            z_at,
            [own, swap(own, z_bits[-1])] + hub_in,
            [((rows, half), BF16)] + hub_out,
        )

    def gather_line(own):
        for mask in z_bits[-2::-1]:
            pair = [own, swap(own, mask)]
            (own,) = run_inside(join_body, z_at, pair, [((2 * own.shape[0], half), BF16)])
        return own

    self_xy = start_sum(feat_t, peer_feat_t, [])
    self_got = across(self_xy[1:], xy_bits)
    agg_pair = in_order([agg_t, peer_agg_t], self_xy)
    neigh_xy = start_sum(*agg_pair, [hub_keep, hub_got])
    neigh_got = across(neigh_xy[1:n_xy], xy_bits)
    self_got = in_order(self_got, [*neigh_xy, counts_own_t])
    (self_own,) = sum_line(self_xy[0], [], self_got)
    neigh_own, hub_back = sum_line(neigh_xy[0], [neigh_xy[n_xy]], neigh_got)

    def place(blocks):
        return run_inside(
            functools.partial(place_body, n_xy, n_z // 2),
            jnp.stack([side, xy_me, z_me]),
            blocks + [swap(one, core) for one in blocks],
            [((width, width), BF16)],
        )[0]

    self_line = gather_line(self_own)
    self_blocks = [self_line] + across([self_line] * (n_xy - 1), xy_bits)
    neigh_line = gather_line(neigh_own)
    (neigh_line,) = in_order([neigh_line], self_blocks)
    neigh_blocks = [neigh_line] + across([neigh_line] * (n_xy - 1), xy_bits)
    grad_self = place(in_order(self_blocks, neigh_blocks[:1]))
    (grad_x,) = run(
        node_body,
        side[None],
        [w_self, d_pre, d_other, counts_own_t, d_agg, chosen, returned, hub_row, hub_back],
        [(wide, BF16)],
        flops=2 * n_local * width * (width + n_local + n_slots),
        limit=VMEM_LIMIT,
    )
    grad_neigh = place(in_order(neigh_blocks, [grad_x, grad_self]))
    return hidden, grad_x, grad_self, grad_neigh


def solution(mesh):
    split = P(AXES, None)
    in_specs = (split, split, P(AXES), split, split, P(AXES), P(), P(), P(), split)
    out_specs = (split, split, P(), P())
    return jax.shard_map(
        on_device, mesh=mesh, in_specs=in_specs, out_specs=out_specs, check_vma=False
    )
```
